512 devices in a mesh: dp: 8 (over z), space: 64 (over x, y, core).
Axes of the slice: x: 4, y: 8, z: 8, core: 2. Of those that a mesh axis runs over, the one named last changes fastest.
Arguments:
- fields: bfloat16 [8, 16, 512, 8, 512], P('dp', None, 'space'), may hold values from -6 to 6
- cotangent: bfloat16 [8, 16, 512, 8, 512], P('dp', None, 'space'), may hold values from -6 to 6
- mode_weight: float32 [16, 16, 64, 64], P(None, None, None, 'space'), may hold values from -1.5 to 1.5
- point_weight: float32 [16, 16], replicated, may hold values from -1.5 to 1.5
- bias_vector: float32 [16], replicated, may hold values from -3 to 3
Outputs:
- grad_fields: bfloat16 [8, 16, 512, 8, 512], P('dp', None, 'space')
- grad_mode: float32 [16, 16, 64, 64], P(None, None, None, 'space')
- grad_point: float32 [16, 16], replicated
- grad_bias: float32 [16], replicated
The draws below stay inside these ranges and needn't reach their ends.
All inputs are finite; a program needn't handle non-finite values.
Results may differ from the reference program's by a relative error of at most 0.015.
Values may be sent and summed in bfloat16 or wider, within the bound.
A program may use at most 64 MiB of HBM per device.

```python
import math
import jax
import jax.numpy as jnp
from jax import lax

C = 16
N = 512
MODES = 64
YW = 8
SAMPLES = 8
CELLS = 16777216


def block_levels(stream_key, shape, pieces, low, top_value):
    def one(position, shards_of):
        heights = jax.random.uniform(jax.random.fold_in(jax.random.fold_in(stream_key, 6), position), (shards_of,), jnp.float32, low / len(pieces), top_value / len(pieces))
        return jnp.repeat(jnp.exp(heights), shape[position] // shards_of).reshape((-1,) + (1,) * (len(shape) - position - 1))

    gain = one(*pieces[0])
    for cut in pieces[1:]:
        gain = gain * one(*cut)
    return gain


def normal_values(stream_key, extent, scale, most, cuts=(), dtype=jnp.bfloat16):
    gain = block_levels(stream_key, extent, cuts, -0.22, 0.18) if cuts else 1.0
    values = jax.random.normal(stream_key, extent, jnp.float32) * scale * gain
    return jnp.minimum(jnp.maximum(values, -most), most).astype(dtype)


def setup_inputs(seed: int = 0) -> dict:
    keys = jax.random.split(jax.random.key(seed), 6)
    return {
        "fields": normal_values(keys[0], (SAMPLES, C, N, YW, N), 1.0, 6.0, ((0, 8), (2, 64))),
        "cotangent": normal_values(keys[1], (SAMPLES, C, N, YW, N), 1.0, 6.0, ((0, 8), (2, 64))),
        "mode_weight": normal_values(keys[2], (C, C, MODES, MODES), 0.25, 1.5, ((3, 64),), jnp.float32),
        "point_weight": normal_values(keys[3], (C, C), C ** -0.5, 1.5, (), jnp.float32),
        "bias_vector": normal_values(keys[4], (C,), 0.5, 3.0, (), jnp.float32),
    }


def basis_table(number, points):
    index = jnp.arange(number).astype(jnp.int32)
    place = jnp.arange(points).astype(jnp.float32)
    half = number // 2
    freq = jnp.where(index < half, index, index - half + 1).astype(jnp.float32)
    angle = 2.0 * math.pi * freq[:, None] * place[None, :] / points
    values = jnp.where((index < half)[:, None], jnp.cos(angle), jnp.sin(angle)) * math.sqrt(2.0 / points)
    values = jnp.where((index == 0)[:, None], jnp.float32(math.sqrt(1.0 / points)) + 0.0 * values, values)
    return values.astype(jnp.bfloat16)

def gelu_slope(value):
    normal_cdf = 0.5 * (1.0 + jax.scipy.special.erf(value / math.sqrt(2.0)))
    density = jnp.exp(-0.5 * value * value) / math.sqrt(2.0 * math.pi)
    return normal_cdf + value * density

def reference(fields, cotangent, mode_weight, point_weight, bias_vector):
    high = lax.Precision.HIGHEST
    table = basis_table(MODES, N).astype(jnp.float32)

    def one_sample(pair):
        sample_in = pair[0].astype(jnp.float32)
        sample_cot = pair[1].astype(jnp.float32)
        depth_u = jnp.einsum('cxyz,kz->cxyk', sample_in, table, precision=high).astype(jnp.bfloat16).astype(jnp.float32)
        spec_u = jnp.einsum('cxyk,jx->kcjy', depth_u, table, precision=high)
        mixing = jnp.einsum('cojk,kcjy->kojy', mode_weight, spec_u, precision=high)
        rows_back = jnp.einsum('kojy,jx->oxyk', mixing, table, precision=high).astype(jnp.bfloat16).astype(jnp.float32)
        pre_act = jnp.einsum('oxyk,kz->oxyz', rows_back, table, precision=high)
        pre_act = pre_act + jnp.einsum('co,cxyz->oxyz', point_weight, sample_in, precision=high) + bias_vector[:, None, None, None]
        grad_pre = (sample_cot * gelu_slope(pre_act)).astype(jnp.bfloat16).astype(jnp.float32)
        depth_g = jnp.einsum('oxyz,kz->oxyk', grad_pre, table, precision=high).astype(jnp.bfloat16).astype(jnp.float32)
        spec_g = jnp.einsum('oxyk,jx->kojy', depth_g, table, precision=high)
        mode_part = jnp.einsum('kcjy,kojy->cojk', spec_u, spec_g, precision=high)
        mode_adj = jnp.einsum('cojk,kojy->kcjy', mode_weight, spec_g, precision=high)
        rows_adj = jnp.einsum('kcjy,jx->cxyk', mode_adj, table, precision=high).astype(jnp.bfloat16).astype(jnp.float32)
        grad_field = jnp.einsum('cxyk,kz->cxyz', rows_adj, table, precision=high)
        grad_field = grad_field + jnp.einsum('co,oxyz->cxyz', point_weight, grad_pre, precision=high)
        point_part = jnp.einsum('cxyz,oxyz->co', sample_in, grad_pre, precision=high)
        bias_part = lax.optimization_barrier(jnp.sum(grad_pre, axis=(1, 2, 3)))
        return (grad_field.astype(jnp.bfloat16), mode_part, point_part, bias_part)
    grad_fields, mode_parts, point_parts, bias_parts = lax.map(one_sample, (fields, cotangent))
    scale_mode = 1.0 / math.sqrt(SAMPLES * YW)
    scale_cell = 1.0 / math.sqrt(CELLS)
    grad_mode = lax.optimization_barrier(jnp.sum(mode_parts, axis=0)) * scale_mode
    grad_point = lax.optimization_barrier(jnp.sum(point_parts, axis=0)) * scale_cell
    grad_bias = lax.optimization_barrier(jnp.sum(bias_parts, axis=0)) * scale_cell
    return (grad_fields, grad_mode, grad_point, grad_bias)
```

```python
import functools
import math

import jax
import jax.numpy as jnp
import ml_dtypes
import numpy as np
from jax import lax
from jax.experimental import pallas as pl
from jax.experimental.pallas import tpu as pltpu
from jax.sharding import PartitionSpec as P

MESH = pl.DeviceIdType.MESH
F32 = jnp.float32
BF16 = jnp.bfloat16


def basis_table(number, points):
    half = number // 2
    index = np.arange(number)
    freq = np.where(index < half, index, index - half + 1)
    angle = 2.0 * math.pi * ((freq[:, None] * np.arange(points)[None, :]) % points) / points
    values = np.where((index < half)[:, None], np.cos(angle), np.sin(angle))
    values = values * math.sqrt(2.0 / points)
    values[0] = math.sqrt(1.0 / points)
    return values.astype(np.float32).astype(ml_dtypes.bfloat16)


ERF_STEP = 0.3275911 / math.sqrt(2.0)
ERF_TERMS = [
    0.5 * a for a in (0.254829592, -0.284496736, 1.421413741, -1.453152027, 1.061405429)
]


def gelu_slope(value):
    size = jnp.abs(value)
    below = 1.0 + ERF_STEP * size
    guess = pl.reciprocal(below, approx=True)
    step = guess * (2.0 - below * guess)
    tail = jnp.full_like(value, ERF_TERMS[4])
    for term in ERF_TERMS[3::-1]:
        tail = tail * step + term
    tail = tail * step
    bell = jnp.exp2(value * value * (-0.5 * math.log2(math.e)))
    rest = bell * (size * (1.0 / math.sqrt(2.0 * math.pi)) - tail)
    return jnp.where(value >= 0.0, 1.0 + rest, -rest)


def dot(a, b, ca, cb, precision=None):
    return lax.dot_general(
        a, b, (((ca,), (cb,)), ((), ())), precision=precision, preferred_element_type=F32
    )


def split(value):
    high = value.astype(BF16)
    low = (value - high.astype(F32)).astype(BF16)
    return high, low


def kernel(
    sizes, fields, cot, weight, point, bias, tz, tx, txt,
    out, gm_out, gp_out, gb_out,
    f_v, c_v, g_v, acc_v, out_v, stage, w2, su_v,
    su_s, su_r, mx_s, mx_r, sg_s, sg_r, ad_s, ad_r,
    gm_s, gm_r, gm_a, pt_r,
    f_sem, c_sem, o_sem, s_sem, r_sem, gs_sem, gr_sem, ps_sem, pr_sem,
):
    S, D, Y, C, XO, YW, Z, J = sizes
    A = S // Y
    CY = C * YW
    H = C // 2
    me = lax.axis_index("space")
    dp = lax.axis_index("dp")

    def f_copy(x):
        return pltpu.make_async_copy(fields.at[0, :, x], f_v.at[x], f_sem.at[x])

    def c_copy(x):
        return pltpu.make_async_copy(cot.at[0, :, x], c_v.at[x], c_sem.at[x])

    def o_copy(x):
        return pltpu.make_async_copy(out_v.at[x], out.at[0, :, x], o_sem.at[x])

    for x in range(XO):
        f_copy(x).start()
    for x in range(XO):
        c_copy(x).start()

    barrier = pltpu.get_barrier_semaphore()

    @pl.loop(1, S)
    def _(i):
        pl.semaphore_signal(
            barrier, inc=1, device_id={"space": lax.rem(me + i, S)}, device_id_type=MESH
        )

    @pl.loop(1, D)
    def _(i):
        pl.semaphore_signal(
            barrier, inc=1, device_id={"dp": lax.rem(dp + i, D)}, device_id_type=MESH
        )

    def send_copy(n, src, dst, to):
        return pltpu.make_async_remote_copy(
            src_ref=src, dst_ref=dst, send_sem=s_sem.at[n], recv_sem=r_sem.at[n],
            device_id={"space": to}, device_id_type=MESH,
        )

    def scatter(n, sent, got):
        @pl.loop(1, S)
        def _(i):
            to = lax.rem(me + i, S)
            send_copy(n, sent.at[to], got.at[me], to).start()

        got[pl.ds(me, 1)] = sent[pl.ds(me, 1)]

    def all_of(n, ref):
        some = ref.at[pl.ds(0, S - 1)]
        return send_copy(n, some, some, lax.rem(me + 1, S))

    def rows_of(ref, x):
        return ref[x].reshape(CY, Z)

    @pl.loop(0, XO)
    def _(x):
        f_copy(x).wait()
        stage[pl.ds(x, S, stride=XO), :] = dot(tz[...], rows_of(f_v, x), 1, 1)

    su_s[...] = stage[...].reshape(S, XO, CY).astype(BF16)
    pl.semaphore_wait(barrier, S + D - 2)
    scatter(0, su_s, su_r)

    for c in range(C):
        w2[c] = jnp.concatenate([weight[c, :H, :], weight[c, H:, :]], axis=-1)
    spread = (
        lax.broadcasted_iota(jnp.int32, (CY, C), 0) // YW
        == lax.broadcasted_iota(jnp.int32, (CY, C), 1)
    )
    spread_f = spread.astype(F32)
    spread_b = spread.astype(BF16)
    same = (
        lax.broadcasted_iota(jnp.int32, (CY, CY), 0) % YW
        == lax.broadcasted_iota(jnp.int32, (CY, CY), 1) % YW
    )

    def kron(part, flip):
        rows = dot(spread_b, part, 1, 0 if not flip else 1).astype(BF16)
        return jnp.where(same, dot(rows, spread_b, 1, 1), 0.0).astype(BF16)

    p_high, p_low = split(point[...])
    into_out = jnp.concatenate([kron(p_high, True), kron(p_low, True)], axis=1)
    into_in = jnp.concatenate([kron(p_high, False), kron(p_low, False)], axis=1)
    bias_col = jnp.sum(spread_f * bias[...], axis=1, keepdims=True)

    @pl.loop(0, XO)
    def _(x):
        rows = rows_of(f_v, x)
        acc_v[x] = dot(into_out, jnp.concatenate([rows, rows], axis=0), 1, 0) + bias_col

    lane = lax.broadcasted_iota(jnp.int32, (H, YW, 2 * J), 2)

    def spectrum(got):
        rows = got[...].reshape(S * XO, CY)
        return dot(tx[...], rows, 1, 0).T.reshape(C, YW, 2 * J)

    def back(values, sent):
        high, low = split(values)
        rows = dot(txt[...], jnp.concatenate([high, low], axis=1), 1, 1)
        sent[...] = rows.reshape(S, XO, CY).astype(BF16)

    all_of(0, su_r).wait_recv()
    su_v[...] = spectrum(su_r)
    mixed = []
    for o in range(H):
        total = w2[0, o : o + 1, :] * su_v[0]
        for c in range(1, C):
            total = total + w2[c, o : o + 1, :] * su_v[c]
        mixed.append(total[None])
    mixed = jnp.concatenate(mixed, axis=0)
    mixed = jnp.concatenate(
        [jnp.where(lane < J, mixed, 0.0), jnp.where(lane >= J, mixed, 0.0)], axis=0
    )
    back(mixed.reshape(CY, 2 * J), mx_s)
    scatter(1, mx_s, mx_r)

    all_of(1, mx_r).wait_recv()
    stage[...] = mx_r[...].astype(F32).reshape(S * XO, CY)
    for x in range(XO):
        c_copy(x).wait()

    def slope_step(x, bias_sum):
        modes = stage[pl.ds(x, S, stride=XO), :].T.astype(BF16)
        pre = acc_v[x] + dot(modes, tz[...], 1, 0)
        grad = (rows_of(c_v, x).astype(F32) * gelu_slope(pre)).astype(BF16)
        g_v[x] = grad
        depth = dot(tz[...], grad, 1, 1)
        stage[pl.ds(x, S, stride=XO), :] = depth
        return bias_sum + depth[0:1, :]

    bias_sum = lax.fori_loop(0, XO, slope_step, jnp.zeros((1, CY), F32))
    sg_s[...] = stage[...].reshape(S, XO, CY).astype(BF16)
    scatter(2, sg_s, sg_r)

    def point_step(x, total):
        rows = g_v[x]
        acc_v[x] = dot(into_in, jnp.concatenate([rows, rows], axis=0), 1, 0)
        return total + dot(rows_of(f_v, x), rows, 1, 1)

    pairs = lax.fori_loop(0, XO, point_step, jnp.zeros((CY, CY), F32))
    pairs = jnp.sum(jnp.where(same, pairs, 0.0).reshape(C, YW, CY), axis=1)
    constant = float(np.float32(ml_dtypes.bfloat16(math.sqrt(1.0 / Z))))
    terms = jnp.concatenate(
        [pairs[:H], pairs[H:], jnp.broadcast_to(bias_sum * (1.0 / constant), (H, CY))], axis=1
    )
    source = lax.broadcasted_iota(jnp.int32, (3 * CY, 128), 0)
    fold = (source // CY) * C + (source % CY) // YW == lax.broadcasted_iota(
        jnp.int32, (3 * CY, 128), 1
    )
    tile = dot(terms, fold.astype(F32), 1, 0, precision=lax.Precision.HIGHEST)

    mine_y = lax.rem(me // 2, Y)
    mine_a = (me // (2 * Y)) * 2 + lax.rem(me, 2)

    def to_a(a):
        return {"space": ((a // 2) * Y + mine_y) * 2 + lax.rem(a, 2)}

    def to_y(y):
        return {"space": ((me // (2 * Y)) * Y + y) * 2 + lax.rem(me, 2)}

    def to_dp(d):
        return {"dp": d}

    rounds = [(0, A, mine_a, to_a, 0), (1, Y, mine_y, to_y, A), (2, D, dp, to_dp, A + Y)]

    def p_copy(n, first, last, place):
        return pltpu.make_async_remote_copy(
            src_ref=first, dst_ref=last, send_sem=ps_sem.at[n], recv_sem=pr_sem.at[n],
            device_id=place, device_id_type=MESH,
        )

    def p_send(n, value):
        _, count, mine, place, base = rounds[n]
        pt_r[pl.ds(base + mine, 1)] = value[None]

        @pl.loop(1, count)
        def _(i):
            slot = pt_r.at[base + mine]
            p_copy(n, slot, slot, place(lax.rem(mine + i, count))).start()

    def p_all(n):
        _, count, mine, place, base = rounds[n]
        some = pt_r.at[pl.ds(base, count - 1)]
        return p_copy(n, some, some, place(lax.rem(mine + 1, count)))

    def p_sum(n):
        _, count, _, _, base = rounds[n]
        p_all(n).wait_recv()
        total = pt_r[base]
        for i in range(1, count):
            total = total + pt_r[base + i]
        return total

    p_send(0, tile)

    all_of(2, sg_r).wait_recv()
    spec = spectrum(sg_r)
    pair = jnp.where(lane < J, spec[:H], spec[H:])
    adjoint = []
    for c in range(C):
        total = w2[c, 0:1, :] * pair[0]
        for o in range(1, H):
            total = total + w2[c, o : o + 1, :] * pair[o]
        adjoint.append(total[None])
    back(jnp.concatenate(adjoint, axis=0).reshape(CY, 2 * J), ad_s)
    scatter(3, ad_s, ad_r)

    part = C // D
    for c in range(C):
        gm_s[c // part, c % part] = jnp.sum(su_v[c][None] * pair, axis=1)

    def g_copy(n, first, last, to):
        return pltpu.make_async_remote_copy(
            src_ref=first, dst_ref=last, send_sem=gs_sem.at[n], recv_sem=gr_sem.at[n],
            device_id={"dp": to}, device_id_type=MESH,
        )

    def g_all(n, ref):
        some = ref.at[pl.ds(0, D - 1)]
        return g_copy(n, some, some, lax.rem(dp + 1, D))

    @pl.loop(1, D)
    def _(i):
        to = lax.rem(dp + i, D)
        g_copy(0, gm_s.at[to], gm_r.at[dp], to).start()

    gm_r[pl.ds(dp, 1)] = gm_s[pl.ds(dp, 1)]
    p_send(1, p_sum(0))
    g_all(0, gm_r).wait_recv()
    total = gm_r[0]
    for i in range(1, D):
        total = total + gm_r[i]
    gm_a[pl.ds(dp, 1)] = (total * (1.0 / math.sqrt(D * YW)))[None]

    @pl.loop(1, D)
    def _(i):
        slot = gm_a.at[dp]
        g_copy(1, slot, slot, lax.rem(dp + i, D)).start()

    p_send(2, p_sum(1))

    all_of(3, ad_r).wait_recv()
    stage[...] = ad_r[...].astype(F32).reshape(S * XO, CY)

    @pl.loop(0, XO)
    def _(x):
        modes = stage[pl.ds(x, S, stride=XO), :].T.astype(BF16)
        grad = acc_v[x] + dot(modes, tz[...], 1, 0)
        out_v[x] = grad.astype(BF16).reshape(C, YW, Z)
        o_copy(x).start()

    final = p_sum(2) * (1.0 / math.sqrt(D * S * XO * YW * Z))
    gp_out[...] = jnp.concatenate([final[:, :C], final[:, C : 2 * C]], axis=0)
    gb_out[...] = final[0:1, 2 * C : 3 * C]
    g_all(1, gm_a).wait_recv()
    for c in range(C):
        value = gm_a[c // part, c % part]
        gm_out[c, :H, :] = value[:, :J]
        gm_out[c, H:, :] = value[:, J:]

    all_of(0, su_s).wait_send()
    all_of(1, mx_s).wait_send()
    all_of(2, sg_s).wait_send()
    all_of(3, ad_s).wait_send()
    for n in range(3):
        p_all(n).wait_send()
    g_all(0, gm_s).wait_send()
    g_all(1, gm_a).wait_send()
    for x in range(XO):
        o_copy(x).wait()


def shards(S, D, fields, cotangent, mode_weight, point_weight, bias_vector):
    _, C, XO, YW, Z = fields.shape
    J = mode_weight.shape[2]
    CY = C * YW
    Y = 8 if S == 64 else 2
    A = S // Y
    H = C // 2
    tz = basis_table(S, Z)
    tx = basis_table(J, S * XO)
    tx = np.concatenate([tx, tx], axis=0)
    txt = np.ascontiguousarray(np.concatenate([tx, tx], axis=0).T)
    block = (S, XO, CY)
    vmem = pl.BlockSpec(memory_space=pltpu.VMEM)
    hbm = pl.BlockSpec(memory_space=pl.ANY)
    dma = pltpu.SemaphoreType.DMA
    grad_fields, grad_mode, grad_point, grad_bias = pl.pallas_call(
        functools.partial(kernel, (S, D, Y, C, XO, YW, Z, J)),
        out_shape=(
            jax.ShapeDtypeStruct(fields.shape, BF16),
            jax.ShapeDtypeStruct((C, C, J), F32),
            jax.ShapeDtypeStruct((C, C), F32),
            jax.ShapeDtypeStruct((1, C), F32),
        ),
        in_specs=[hbm, hbm, vmem, vmem, vmem, vmem, vmem, vmem],
        out_specs=(hbm, vmem, vmem, vmem),
        scratch_shapes=[
            pltpu.VMEM((XO, C, YW, Z), BF16),
            pltpu.VMEM((XO, C, YW, Z), BF16),
            pltpu.VMEM((XO, CY, Z), BF16),
            pltpu.VMEM((XO, CY, Z), F32),
            pltpu.VMEM((XO, C, YW, Z), BF16),
            pltpu.VMEM((S * XO, CY), F32),
            pltpu.VMEM((C, H, 2 * J), F32),
            pltpu.VMEM((C, YW, 2 * J), F32),
        ]
        + [pltpu.VMEM(block, BF16)] * 8
        + [
            pltpu.VMEM((D, C // D, H, 2 * J), F32),
            pltpu.VMEM((D, C // D, H, 2 * J), F32),
            pltpu.VMEM((D, C // D, H, 2 * J), F32),
            pltpu.VMEM((A + Y + D, 8, 128), F32),
            dma((XO,)),
            dma((XO,)),
            dma((XO,)),
            dma((4,)),
            dma((4,)),
            dma((2,)),
            dma((2,)),
            dma((3,)),
            dma((3,)),
        ],
        compiler_params=pltpu.CompilerParams(
            collective_id=0, has_side_effects=True, vmem_limit_bytes=32 * 1024 * 1024
        ),
    )(
        fields,
        cotangent,
        mode_weight.reshape(C, C, J),
        point_weight,
        bias_vector.reshape(1, C),
        tz,
        tx,
        txt,
    )
    return (
        grad_fields,
        grad_mode.reshape(mode_weight.shape),
        grad_point,
        grad_bias.reshape(C),
    )


def solution(mesh):
    return jax.shard_map(
        functools.partial(shards, mesh.shape["space"], mesh.shape["dp"]),
        mesh=mesh,
        in_specs=(
            P("dp", None, "space", None, None),
            P("dp", None, "space", None, None),
            P(None, None, None, "space"),
            P(),
            P(),
        ),
        out_specs=(P("dp", None, "space", None, None), P(None, None, None, "space"), P(), P()),
        check_vma=False,
    )
```

```python
import functools
import math

import jax
import jax.numpy as jnp
import ml_dtypes
import numpy as np
from jax import lax
from jax.experimental import pallas as pl
from jax.experimental.pallas import tpu as pltpu
from jax.sharding import PartitionSpec as P

MESH = pl.DeviceIdType.MESH
F32 = jnp.float32
BF16 = jnp.bfloat16


def basis_table(number, points):
    half = number // 2
    index = np.arange(number)
    freq = np.where(index < half, index, index - half + 1)
    angle = 2.0 * math.pi * ((freq[:, None] * np.arange(points)[None, :]) % points) / points
    values = np.where((index < half)[:, None], np.cos(angle), np.sin(angle))
    values = values * math.sqrt(2.0 / points)
    values[0] = math.sqrt(1.0 / points)
    return values.astype(np.float32).astype(ml_dtypes.bfloat16)


def gelu_slope(value):
    scaled = value * math.sqrt(0.5)
    bell = jnp.exp2(scaled * scaled * (-math.log2(math.e)))
    return 0.5 + 0.5 * lax.erf(scaled) + scaled * (bell * (1.0 / math.sqrt(math.pi)))


def dot(a, b, ca, cb, precision=None):
    return lax.dot_general(
        a, b, (((ca,), (cb,)), ((), ())), precision=precision, preferred_element_type=F32
    )


def split(value):
    high = value.astype(BF16)
    low = (value - high.astype(F32)).astype(BF16)
    return high, low


def layer_kernel(
    sizes, fields, cot, weight_in, point_in, bias_in, tz_in, tx_in, txt_in,
    acc_v, ad_out, su_out, sg_out, sum_out, tz,
    f_v, c_v, g_v, stage, w2, weight, point, bias, tx, txt,
    su_s, su_r, mx_s, mx_r, sg_s, sg_r, ad_s, ad_r,
    du_r, dg_r, pt_r,
    f_sem, c_sem, i_sem, s_sem, r_sem, gs_sem, gr_sem, ps_sem, pr_sem,
):
    S, D, Y, C, XO, YW, Z, J = sizes
    A = S // Y
    X = A // 2
    CY = C * YW
    H = C // 2
    me = lax.axis_index("space")
    dp = lax.axis_index("dp")
    mine_x = me // (2 * Y)
    mine_y = lax.rem(me // 2, Y)
    mine_c = lax.rem(me, 2)

    def f_copy(x):
        return pltpu.make_async_copy(fields.at[0, :, x], f_v.at[x], f_sem.at[x])

    def c_copy(x):
        return pltpu.make_async_copy(cot.at[0, :, x], c_v.at[x], c_sem.at[x])

    small = [
        pltpu.make_async_copy(src, dst, i_sem.at[n])
        for n, (src, dst) in enumerate(
            [(tz_in, tz), (tx_in, tx), (txt_in, txt), (weight_in, weight),
             (point_in, point), (bias_in, bias)]
        )
    ]
    small[0].start()
    for x in range(XO):
        f_copy(x).start()

    def far_first(i):
        n, m = i // A, lax.rem(i // 2, X)
        step_y = Y + Y // 2 + ((n + 1) // 2) * (1 - 2 * lax.rem(n, 2))
        step_x = X + X // 2 + ((m + 1) // 2) * (1 - 2 * lax.rem(m, 2))
        to_x = lax.rem(mine_x + step_x, X)
        to_y = lax.rem(mine_y + step_y, Y)
        to_c = lax.rem(mine_c + 1 - lax.rem(i, 2), 2)
        return (to_x * Y + to_y) * 2 + to_c

    barrier = pltpu.get_barrier_semaphore()

    @pl.loop(0, S - 1)
    def _(i):
        pl.semaphore_signal(
            barrier, inc=1, device_id={"space": far_first(i)}, device_id_type=MESH
        )

    @pl.loop(1, D)
    def _(i):
        pl.semaphore_signal(
            barrier, inc=1, device_id={"dp": lax.rem(dp + i, D)}, device_id_type=MESH
        )

    for copy in small[1:]:
        copy.start()
    for x in range(XO):
        c_copy(x).start()

    def send_copy(n, src, dst, to):
        return pltpu.make_async_remote_copy(
            src_ref=src, dst_ref=dst, send_sem=s_sem.at[n], recv_sem=r_sem.at[n],
            device_id={"space": to}, device_id_type=MESH,
        )

    def scatter(n, sent, got):
        @pl.loop(0, S - 1)
        def _(i):
            to = far_first(i)
            send_copy(n, sent.at[to], got.at[me], to).start()

        got[pl.ds(me, 1)] = sent[pl.ds(me, 1)]

    def all_of(n, ref):
        some = ref.at[pl.ds(0, S - 1)]
        return send_copy(n, some, some, lax.rem(me + 1, S))

    def gather_copy(n, ref, to):
        return pltpu.make_async_remote_copy(
            src_ref=ref, dst_ref=ref, send_sem=gs_sem.at[n], recv_sem=gr_sem.at[n],
            device_id={"dp": to}, device_id_type=MESH,
        )

    def gather(n, ref, value):
        ref[pl.ds(dp, 1)] = value[None]

        @pl.loop(1, D)
        def _(i):
            gather_copy(n, ref.at[dp], lax.rem(dp + i, D)).start()

    def gather_all(n, ref):
        return gather_copy(n, ref.at[pl.ds(0, D - 1)], lax.rem(dp + 1, D))

    def rows_of(ref, x):
        return ref[x].reshape(CY, Z)

    small[0].wait()
    for x in range(XO):
        f_copy(x).wait()
        stage[pl.ds(x, S, stride=XO), :] = dot(tz[...], rows_of(f_v, x), 1, 1)
    su_s[...] = stage[...].reshape(S, XO, CY).astype(BF16)
    pl.semaphore_wait(barrier, S + D - 2)
    scatter(0, su_s, su_r)

    for copy in small[1:]:
        copy.wait()
    for c in range(C):
        w2[c] = jnp.concatenate([weight[c, :H, :], weight[c, H:, :]], axis=-1)
    spread = (
        lax.broadcasted_iota(jnp.int32, (CY, C), 0) // YW
        == lax.broadcasted_iota(jnp.int32, (CY, C), 1)
    )
    spread_f = spread.astype(F32)
    spread_b = spread.astype(BF16)
    same = (
        lax.broadcasted_iota(jnp.int32, (CY, CY), 0) % YW
        == lax.broadcasted_iota(jnp.int32, (CY, CY), 1) % YW
    )

    def kron(part, flip):
        rows = dot(spread_b, part, 1, 0 if not flip else 1).astype(BF16)
        return jnp.where(same, dot(rows, spread_b, 1, 1), 0.0).astype(BF16)

    p_high, p_low = split(point[...])
    into_out = jnp.concatenate([kron(p_high, True), kron(p_low, True)], axis=1)
    into_in = jnp.concatenate([kron(p_high, False), kron(p_low, False)], axis=1)
    bias_col = jnp.sum(spread_f * bias[...], axis=1, keepdims=True)

    for x in range(XO):
        rows = rows_of(f_v, x)
        acc_v[x] = dot(into_out, jnp.concatenate([rows, rows], axis=0), 1, 0) + bias_col

    lane = lax.broadcasted_iota(jnp.int32, (H, YW, 2 * J), 2)

    def spectrum(got):
        rows = got[...].reshape(S * XO, CY)
        return dot(tx[...], rows, 1, 0).T.reshape(C, YW, 2 * J)

    def back(values, sent):
        high, low = split(values)
        rows = dot(txt[...], jnp.concatenate([high, low], axis=1), 1, 1)
        sent[...] = rows.reshape(S, XO, CY).astype(BF16)

    all_of(0, su_r).wait_recv()
    spec_u = spectrum(su_r)
    mixed = []
    for o in range(H):
        total = w2[0, o : o + 1, :] * spec_u[0]
        for c in range(1, C):
            total = total + w2[c, o : o + 1, :] * spec_u[c]
        mixed.append(total[None])
    mixed = jnp.concatenate(mixed, axis=0)
    mixed = jnp.concatenate(
        [jnp.where(lane < J, mixed, 0.0), jnp.where(lane >= J, mixed, 0.0)], axis=0
    )
    back(mixed.reshape(CY, 2 * J), mx_s)
    scatter(1, mx_s, mx_r)
    gather(0, du_r, spec_u.astype(BF16))

    all_of(1, mx_r).wait_recv()
    stage[...] = mx_r[...].astype(F32).reshape(S * XO, CY)
    for x in range(XO):
        c_copy(x).wait()

    def slope_step(x, bias_sum):
        modes = stage[pl.ds(x, S, stride=XO), :].T.astype(BF16)
        pre = acc_v[x] + dot(modes, tz[...], 1, 0)
        grad = (rows_of(c_v, x).astype(F32) * gelu_slope(pre)).astype(BF16)
        g_v[x] = grad
        depth = dot(tz[...], grad, 1, 1)
        stage[pl.ds(x, S, stride=XO), :] = depth
        return bias_sum + depth[0:1, :]

    bias_sum = jnp.zeros((1, CY), F32)
    for x in range(XO):
        bias_sum = slope_step(x, bias_sum)
    sg_s[...] = stage[...].reshape(S, XO, CY).astype(BF16)
    scatter(2, sg_s, sg_r)

    pairs = jnp.zeros((CY, CY), F32)
    for x in range(XO):
        pairs = pairs + dot(rows_of(f_v, x), g_v[x], 1, 1)
    pairs = jnp.sum(jnp.where(same, pairs, 0.0).reshape(C, YW, CY), axis=1)
    constant = float(np.float32(ml_dtypes.bfloat16(math.sqrt(1.0 / Z))))
    terms = jnp.concatenate(
        [pairs[:H], pairs[H:], jnp.broadcast_to(bias_sum * (1.0 / constant), (H, CY))], axis=1
    )
    source = lax.broadcasted_iota(jnp.int32, (3 * CY, 128), 0)
    fold = (source // CY) * C + (source % CY) // YW == lax.broadcasted_iota(
        jnp.int32, (3 * CY, 128), 1
    )
    tile = dot(terms, fold.astype(F32), 1, 0, precision=lax.Precision.HIGHEST)

    mine_a = mine_x * 2 + mine_c

    def to_a(a):
        return {"space": ((a // 2) * Y + mine_y) * 2 + lax.rem(a, 2)}

    def to_y(y):
        return {"space": (mine_x * Y + y) * 2 + mine_c}

    def to_dp(d):
        return {"dp": d}

    rounds = [(0, A, mine_a, to_a, 0), (1, Y, mine_y, to_y, A), (2, D, dp, to_dp, A + Y)]

    def p_copy(n, first, last, place):
        return pltpu.make_async_remote_copy(
            src_ref=first, dst_ref=last, send_sem=ps_sem.at[n], recv_sem=pr_sem.at[n],
            device_id=place, device_id_type=MESH,
        )

    def p_send(n, value):
        _, count, mine, place, base = rounds[n]
        pt_r[pl.ds(base + mine, 1)] = value[None]

        @pl.loop(1, count)
        def _(i):
            slot = pt_r.at[base + mine]
            p_copy(n, slot, slot, place(lax.rem(mine + i, count))).start()

    def p_all(n):
        _, count, mine, place, base = rounds[n]
        some = pt_r.at[pl.ds(base, count - 1)]
        return p_copy(n, some, some, place(lax.rem(mine + 1, count)))

    def p_sum(n):
        _, count, _, _, base = rounds[n]
        p_all(n).wait_recv()
        total = pt_r[base]
        for i in range(1, count):
            total = total + pt_r[base + i]
        return total

    p_send(0, tile)
    for x in range(XO):
        rows = g_v[x]
        acc_v[x] = dot(into_in, jnp.concatenate([rows, rows], axis=0), 1, 0)
    gather_all(0, du_r).wait_recv()
    su_out[...] = du_r[...]
    p_send(1, p_sum(0))

    all_of(2, sg_r).wait_recv()
    spec = spectrum(sg_r)
    pair = jnp.where(lane < J, spec[:H], spec[H:])
    adjoint = []
    for c in range(C):
        total = w2[c, 0:1, :] * pair[0]
        for o in range(1, H):
            total = total + w2[c, o : o + 1, :] * pair[o]
        adjoint.append(total[None])
    back(jnp.concatenate(adjoint, axis=0).reshape(CY, 2 * J), ad_s)
    scatter(3, ad_s, ad_r)
    gather(1, dg_r, pair.astype(BF16))
    p_send(2, p_sum(1))

    all_of(3, ad_r).wait_recv()
    ad_out[...] = ad_r[...]
    gather_all(1, dg_r).wait_recv()
    sg_out[...] = dg_r[...]
    sum_out[...] = p_sum(2)

    all_of(0, su_s).wait_send()
    all_of(1, mx_s).wait_send()
    all_of(2, sg_s).wait_send()
    all_of(3, ad_s).wait_send()
    for n in range(3):
        p_all(n).wait_send()
    gather_all(0, du_r).wait_send()
    gather_all(1, dg_r).wait_send()


def result_kernel(
    sizes, acc, ad, su, sg, sums, tz,
    out, gm_out, gp_out, gb_out,
    out_v, stage, sg_v, gm_v, gp_v, gb_v, o_sem, g_sem,
):
    S, D, Y, C, XO, YW, Z, J = sizes
    CY = C * YW
    H = C // 2

    def o_copy(x):
        return pltpu.make_async_copy(out_v.at[x], out.at[0, :, x], o_sem.at[x])

    stage[...] = ad[...].astype(F32).reshape(S * XO, CY)
    for x in range(XO):
        modes = stage[pl.ds(x, S, stride=XO), :].T.astype(BF16)
        grad = acc[x] + dot(modes, tz[...], 1, 0)
        out_v[x] = grad.astype(BF16).reshape(C, YW, Z)
        o_copy(x).start()

    final = sums[...] * (1.0 / math.sqrt(D * S * XO * YW * Z))
    gp_v[...] = jnp.concatenate([final[:, :C], final[:, C : 2 * C]], axis=0)
    gb_v[...] = final[0:1, 2 * C : 3 * C]
    sg_v[...] = sg[...].astype(F32) * (1.0 / math.sqrt(D * YW))
    for c in range(C):
        total = su[0, c].astype(F32)[None] * sg_v[0]
        for d in range(1, D):
            total = total + su[d, c].astype(F32)[None] * sg_v[d]
        total = jnp.sum(total, axis=1)
        gm_v[c, :H, :] = total[:, :J]
        gm_v[c, H:, :] = total[:, J:]
    copies = [
        pltpu.make_async_copy(src, dst, g_sem.at[n])
        for n, (src, dst) in enumerate([(gm_v, gm_out), (gp_v, gp_out), (gb_v, gb_out)])
    ]
    for copy in copies:
        copy.start()
    for x in range(XO):
        o_copy(x).wait()
    for copy in copies:
        copy.wait()


def shards(S, D, fields, cotangent, mode_weight, point_weight, bias_vector):
    _, C, XO, YW, Z = fields.shape
    J = mode_weight.shape[2]
    CY = C * YW
    Y = 8 if S == 64 else 2
    A = S // Y
    H = C // 2
    tz = basis_table(S, Z)
    tx = basis_table(J, S * XO)
    tx = np.concatenate([tx, tx], axis=0)
    txt = np.ascontiguousarray(np.concatenate([tx, tx], axis=0).T)
    sizes = (S, D, Y, C, XO, YW, Z, J)
    block = (S, XO, CY)
    vmem = pl.BlockSpec(memory_space=pltpu.VMEM)
    hbm = pl.BlockSpec(memory_space=pltpu.HBM)
    dma = pltpu.SemaphoreType.DMA
    shape = jax.ShapeDtypeStruct
    held = pl.pallas_call(
        functools.partial(layer_kernel, sizes),
        out_shape=(
            shape((XO, CY, Z), F32),
            shape(block, BF16),
            shape((D, C, YW, 2 * J), BF16),
            shape((D, H, YW, 2 * J), BF16),
            shape((H, 128), F32),
            shape((S, Z), BF16),
        ),
        in_specs=[hbm] * 8,
        out_specs=(vmem,) * 6,
        scratch_shapes=[
            pltpu.VMEM((XO, C, YW, Z), BF16),
            pltpu.VMEM((XO, C, YW, Z), BF16),
            pltpu.VMEM((XO, CY, Z), BF16),
            pltpu.VMEM((S * XO, CY), F32),
            pltpu.VMEM((C, H, 2 * J), F32),
            pltpu.VMEM((C, C, J), F32),
            pltpu.VMEM((C, C), F32),
            pltpu.VMEM((1, C), F32),
            pltpu.VMEM((2 * J, S * XO), BF16),
            pltpu.VMEM((S * XO, 4 * J), BF16),
        ]
        + [pltpu.VMEM(block, BF16)] * 8
        + [
            pltpu.VMEM((D, C, YW, 2 * J), BF16),
            pltpu.VMEM((D, H, YW, 2 * J), BF16),
            pltpu.VMEM((A + Y + D, H, 128), F32),
            dma((XO,)),
            dma((XO,)),
            dma((6,)),
            dma((4,)),
            dma((4,)),
            dma((2,)),
            dma((2,)),
            dma((3,)),
            dma((3,)),
        ],
        compiler_params=pltpu.CompilerParams(
            collective_id=0, has_side_effects=True, vmem_limit_bytes=24 * 1024 * 1024
        ),
    )(
        *(
            pltpu.with_memory_space_constraint(operand, pltpu.HBM)
            for operand in (
                fields,
                cotangent,
                mode_weight.reshape(C, C, J),
                point_weight,
                bias_vector.reshape(1, C),
                jnp.asarray(tz),
                jnp.asarray(tx),
                jnp.asarray(txt),
            )
        )
    )
    grad_fields, grad_mode, grad_point, grad_bias = pl.pallas_call(
        functools.partial(result_kernel, sizes),
        out_shape=(
            shape(fields.shape, BF16),
            shape((C, C, J), F32),
            shape((C, C), F32),
            shape((1, C), F32),
        ),
        in_specs=[vmem] * 6,
        out_specs=(hbm,) * 4,
        scratch_shapes=[
            pltpu.VMEM((XO, C, YW, Z), BF16),
            pltpu.VMEM((S * XO, CY), F32),
            pltpu.VMEM((D, H, YW, 2 * J), F32),
            pltpu.VMEM((C, C, J), F32),
            pltpu.VMEM((C, C), F32),
            pltpu.VMEM((1, C), F32),
            dma((XO,)),
            dma((3,)),
        ],
        compiler_params=pltpu.CompilerParams(vmem_limit_bytes=24 * 1024 * 1024),
    )(*held)
    return (
        grad_fields,
        grad_mode.reshape(mode_weight.shape),
        grad_point,
        grad_bias.reshape(C),
    )


def solution(mesh):
    return jax.shard_map(
        functools.partial(shards, mesh.shape["space"], mesh.shape["dp"]),
        mesh=mesh,
        in_specs=(
            P("dp", None, "space", None, None),
            P("dp", None, "space", None, None),
            P(None, None, None, "space"),
            P(),
            P(),
        ),
        out_specs=(P("dp", None, "space", None, None), P(None, None, None, "space"), P(), P()),
        check_vma=False,
    )
```

```python
import functools
import math

import jax
import jax.numpy as jnp
import ml_dtypes
import numpy as np
from jax import lax
from jax.experimental import pallas as pl
from jax.experimental.pallas import tpu as pltpu
from jax.sharding import PartitionSpec as P

MESH = pl.DeviceIdType.MESH
F32 = jnp.float32
BF16 = jnp.bfloat16


def basis_table(number, points):
    half = number // 2
    index = np.arange(number)
    freq = np.where(index < half, index, index - half + 1)
    angle = 2.0 * math.pi * ((freq[:, None] * np.arange(points)[None, :]) % points) / points
    values = np.where((index < half)[:, None], np.cos(angle), np.sin(angle))
    values = values * math.sqrt(2.0 / points)
    values[0] = math.sqrt(1.0 / points)
    return values.astype(np.float32).astype(ml_dtypes.bfloat16)


def gelu_slope(value):
    scaled = value * math.sqrt(0.5)
    bell = jnp.exp2(scaled * scaled * (-math.log2(math.e)))
    return 0.5 + 0.5 * lax.erf(scaled) + scaled * (bell * (1.0 / math.sqrt(math.pi)))


def dot(a, b, ca, cb, precision=None):
    return lax.dot_general(
        a, b, (((ca,), (cb,)), ((), ())), precision=precision, preferred_element_type=F32
    )


def split(value):
    high = value.astype(BF16)
    low = (value - high.astype(F32)).astype(BF16)
    return high, low


def layer_kernel(
    sizes, fields, cot, weight_in, point_in, bias_in, tz_in, tx_in, txt_in,
    acc_v, ad_out, su_out, sg_out, sum_out, tz,
    f_v, c_v, g_v, stage, w2, weight, point, bias, tx, txt,
    su_s, su_r, mx_s, mx_r, sg_s, sg_r, ad_s, ad_r,
    du_r, dg_r, pt_r,
    f_sem, c_sem, i_sem, s_sem, r_sem, gs_sem, gr_sem, ps_sem, pr_sem,
):
    S, D, Y, C, XO, YW, Z, J, Q = sizes
    A = S // Y
    X = A // 2
    R = XO // Q
    CY = C * YW
    H = C // 2
    me = lax.axis_index("space")
    dp = lax.axis_index("dp")
    mine_x = me // (2 * Y)
    mine_y = lax.rem(me // 2, Y)
    mine_c = lax.rem(me, 2)

    def f_copy(x):
        return pltpu.make_async_copy(fields.at[0, :, x], f_v.at[x], f_sem.at[x])

    def c_copy(x):
        return pltpu.make_async_copy(cot.at[0, :, x], c_v.at[x], c_sem.at[x])

    small = [
        pltpu.make_async_copy(src, dst, i_sem.at[n])
        for n, (src, dst) in enumerate(
            [(tz_in, tz), (tx_in, tx), (txt_in, txt), (weight_in, weight),
             (point_in, point), (bias_in, bias)]
        )
    ]
    small[0].start()
    for x in range(XO):
        f_copy(x).start()

    def far_first(act):
        classes = [(a, b) for a in range(X // 2 + 1) for b in range(Y // 2 + 1)]
        for a, b in sorted(classes, key=lambda hops: -sum(hops)):
            ways_x = 1 if 2 * a % X == 0 else 2
            ways_y = 1 if 2 * b % Y == 0 else 2

            @pl.loop(0, 2 * ways_x * ways_y if a + b else 1)
            def _(i):
                turn_x = lax.rem(i // 2, ways_x)
                turn_y = i // (2 * ways_x)
                to_x = lax.rem(mine_x + a + turn_x * (X - 2 * a), X)
                to_y = lax.rem(mine_y + b + turn_y * (Y - 2 * b), Y)
                to_c = lax.rem(mine_c + 1 + lax.rem(i, 2), 2)
                act((to_x * Y + to_y) * 2 + to_c)

    barrier = pltpu.get_barrier_semaphore()

    @far_first
    def _(to):
        pl.semaphore_signal(barrier, inc=1, device_id={"space": to}, device_id_type=MESH)

    @pl.loop(1, D)
    def _(i):
        pl.semaphore_signal(
            barrier, inc=1, device_id={"dp": lax.rem(dp + i, D)}, device_id_type=MESH
        )

    for copy in small[1:]:
        copy.start()
    for x in range(XO):
        c_copy(x).start()

    def send_copy(n, src, dst, to):
        return pltpu.make_async_remote_copy(
            src_ref=src, dst_ref=dst, send_sem=s_sem.at[n], recv_sem=r_sem.at[n],
            device_id={"space": to}, device_id_type=MESH,
        )

    def scatter(n, q, sent, got):
        @far_first
        def _(to):
            send_copy(n * Q + q, sent.at[q, to], got.at[q, me], to).start()

        got[q, pl.ds(me, 1)] = sent[q, pl.ds(me, 1)]

    def all_of(n, q, ref):
        some = ref.at[q, pl.ds(0, S - 1)]
        return send_copy(n * Q + q, some, some, lax.rem(me + 1, S))

    def gather_copy(n, ref, to):
        return pltpu.make_async_remote_copy(
            src_ref=ref, dst_ref=ref, send_sem=gs_sem.at[n], recv_sem=gr_sem.at[n],
            device_id={"dp": to}, device_id_type=MESH,
        )

    def gather(n, ref, value):
        ref[pl.ds(dp, 1)] = value[None]

        @pl.loop(1, D)
        def _(i):
            gather_copy(n, ref.at[dp], lax.rem(dp + i, D)).start()

    def gather_all(n, ref):
        return gather_copy(n, ref.at[pl.ds(0, D - 1)], lax.rem(dp + 1, D))

    def rows_of(ref, x):
        return ref[x].reshape(CY, Z)

    small[0].wait()
    for q in range(Q):
        for r in range(R):
            f_copy(q * R + r).wait()
            stage[q, pl.ds(r, S, stride=R), :] = dot(tz[...], rows_of(f_v, q * R + r), 1, 1)
        su_s[q] = stage[q].astype(BF16).reshape(S, R, CY)
        if q == 0:
            pl.semaphore_wait(barrier, S + D - 2)
        scatter(0, q, su_s, su_r)

    for copy in small[1:]:
        copy.wait()
    for c in range(C):
        w2[c] = jnp.concatenate([weight[c, :H, :], weight[c, H:, :]], axis=-1)
    spread = (
        lax.broadcasted_iota(jnp.int32, (CY, C), 0) // YW
        == lax.broadcasted_iota(jnp.int32, (CY, C), 1)
    )
    spread_f = spread.astype(F32)
    spread_b = spread.astype(BF16)
    same = (
        lax.broadcasted_iota(jnp.int32, (CY, CY), 0) % YW
        == lax.broadcasted_iota(jnp.int32, (CY, CY), 1) % YW
    )

    def kron(part, flip):
        rows = dot(spread_b, part, 1, 0 if not flip else 1).astype(BF16)
        return jnp.where(same, dot(rows, spread_b, 1, 1), 0.0).astype(BF16)

    p_high, p_low = split(point[...])
    into_out = jnp.concatenate([kron(p_high, True), kron(p_low, True)], axis=1)
    into_in = jnp.concatenate([kron(p_high, False), kron(p_low, False)], axis=1)
    bias_col = jnp.sum(spread_f * bias[...], axis=1, keepdims=True)

    for x in range(XO):
        rows = rows_of(f_v, x)
        acc_v[x] = dot(into_out, jnp.concatenate([rows, rows], axis=0), 1, 0) + bias_col

    lane = lax.broadcasted_iota(jnp.int32, (H, YW, 2 * J), 2)

    def spectrum(got):
        rows = got[...].reshape(Q * S * R, CY)
        return dot(tx[...], rows, 1, 0).T.reshape(C, YW, 2 * J)

    def back(values):
        high, low = split(values)
        rows = dot(txt[...], jnp.concatenate([high, low], axis=1), 1, 1)
        return rows.astype(BF16).reshape(Q, S, R, CY)

    for q in range(Q):
        all_of(0, q, su_r).wait_recv()
    spec_u = spectrum(su_r)
    mixed = []
    for o in range(H):
        total = w2[0, o : o + 1, :] * spec_u[0]
        for c in range(1, C):
            total = total + w2[c, o : o + 1, :] * spec_u[c]
        mixed.append(total[None])
    mixed = jnp.concatenate(mixed, axis=0)
    mixed = jnp.concatenate(
        [jnp.where(lane < J, mixed, 0.0), jnp.where(lane >= J, mixed, 0.0)], axis=0
    )
    mx_s[...] = back(mixed.reshape(CY, 2 * J))
    for q in range(Q):
        scatter(1, q, mx_s, mx_r)
    gather(0, du_r, jnp.where(lane < J, spec_u[:H], spec_u[H:]).astype(BF16))

    bias_sum = jnp.zeros((1, CY), F32)
    for q in range(Q):
        all_of(1, q, mx_r).wait_recv()
        stage[q] = mx_r[q].reshape(S * R, CY).astype(F32)
        if q == 0:
            for x in range(XO):
                c_copy(x).wait()
        for r in range(R):
            x = q * R + r
            modes = stage[q, pl.ds(r, S, stride=R), :].T.astype(BF16)
            pre = acc_v[x] + dot(modes, tz[...], 1, 0)
            grad = (rows_of(c_v, x).astype(F32) * gelu_slope(pre)).astype(BF16)
            g_v[x] = grad
            depth = dot(tz[...], grad, 1, 1)
            stage[q, pl.ds(r, S, stride=R), :] = depth
            bias_sum = bias_sum + depth[0:1, :]
        sg_s[q] = stage[q].astype(BF16).reshape(S, R, CY)
        scatter(2, q, sg_s, sg_r)

    pairs = jnp.zeros((CY, CY), F32)
    for x in range(XO):
        pairs = pairs + dot(rows_of(f_v, x), g_v[x], 1, 1)
    pairs = jnp.sum(jnp.where(same, pairs, 0.0).reshape(C, YW, CY), axis=1)
    constant = float(np.float32(ml_dtypes.bfloat16(math.sqrt(1.0 / Z))))
    terms = jnp.concatenate(
        [pairs[:H], pairs[H:], jnp.broadcast_to(bias_sum * (1.0 / constant), (H, CY))], axis=1
    )
    source = lax.broadcasted_iota(jnp.int32, (3 * CY, 128), 0)
    fold = (source // CY) * C + (source % CY) // YW == lax.broadcasted_iota(
        jnp.int32, (3 * CY, 128), 1
    )
    tile = dot(terms, fold.astype(F32), 1, 0, precision=lax.Precision.HIGHEST)

    mine_a = mine_x * 2 + mine_c

    def to_a(a):
        return {"space": ((a // 2) * Y + mine_y) * 2 + lax.rem(a, 2)}

    def to_y(y):
        return {"space": (mine_x * Y + y) * 2 + mine_c}

    def to_dp(d):
        return {"dp": d}

    rounds = [(0, A, mine_a, to_a, 0), (1, Y, mine_y, to_y, A), (2, D, dp, to_dp, A + Y)]

    def p_copy(n, first, last, place):
        return pltpu.make_async_remote_copy(
            src_ref=first, dst_ref=last, send_sem=ps_sem.at[n], recv_sem=pr_sem.at[n],
            device_id=place, device_id_type=MESH,
        )

    def p_send(n, value):
        _, count, mine, place, base = rounds[n]
        pt_r[pl.ds(base + mine, 1)] = value[None]

        @pl.loop(1, count)
        def _(i):
            slot = pt_r.at[base + mine]
            p_copy(n, slot, slot, place(lax.rem(mine + i, count))).start()

    def p_all(n):
        _, count, mine, place, base = rounds[n]
        some = pt_r.at[pl.ds(base, count - 1)]
        return p_copy(n, some, some, place(lax.rem(mine + 1, count)))

    def p_sum(n):
        _, count, _, _, base = rounds[n]
        p_all(n).wait_recv()
        total = pt_r[base]
        for i in range(1, count):
            total = total + pt_r[base + i]
        return total

    p_send(0, tile)
    for x in range(XO):
        rows = g_v[x]
        acc_v[x] = dot(into_in, jnp.concatenate([rows, rows], axis=0), 1, 0)
    gather_all(0, du_r).wait_recv()
    su_out[...] = du_r[...]
    p_send(1, p_sum(0))

    for q in range(Q):
        all_of(2, q, sg_r).wait_recv()
    spec = spectrum(sg_r)
    pair = jnp.where(lane < J, spec[:H], spec[H:])
    gather(1, dg_r, pair.astype(BF16))
    adjoint = []
    for c in range(C):
        total = w2[c, 0:1, :] * pair[0]
        for o in range(1, H):
            total = total + w2[c, o : o + 1, :] * pair[o]
        adjoint.append(total[None])
    ad_s[...] = back(jnp.concatenate(adjoint, axis=0).reshape(CY, 2 * J))
    for q in range(Q):
        scatter(3, q, ad_s, ad_r)
    p_send(2, p_sum(1))

    for q in range(Q):
        all_of(3, q, ad_r).wait_recv()
    ad_out[...] = ad_r[...]
    gather_all(1, dg_r).wait_recv()
    sg_out[...] = dg_r[...]
    sum_out[...] = p_sum(2)

    for q in range(Q):
        for n, sent in enumerate([su_s, mx_s, sg_s, ad_s]):
            all_of(n, q, sent).wait_send()
    for n in range(3):
        p_all(n).wait_send()
    gather_all(0, du_r).wait_send()
    gather_all(1, dg_r).wait_send()


def result_kernel(
    sizes, acc, ad, su, sg, sums, tz,
    out, gm_out, gp_out, gb_out,
    out_v, stage, sg_v, gm_v, gp_v, gb_v, o_sem, g_sem,
):
    S, D, Y, C, XO, YW, Z, J, Q = sizes
    CY = C * YW
    H = C // 2
    R = XO // Q
    low = lax.broadcasted_iota(jnp.int32, (YW, 2 * J), 1) < J

    def o_copy(x):
        return pltpu.make_async_copy(out_v.at[x], out.at[0, :, x], o_sem.at[x])

    stage[...] = ad[...].reshape(Q, S * R, CY).astype(F32)
    for x in range(XO):
        modes = stage[x // R, pl.ds(x % R, S, stride=R), :].T.astype(BF16)
        grad = acc[x] + dot(modes, tz[...], 1, 0)
        out_v[x] = grad.astype(BF16).reshape(C, YW, Z)
        o_copy(x).start()

    final = sums[...] * (1.0 / math.sqrt(D * S * XO * YW * Z))
    gp_v[...] = jnp.concatenate([final[:, :C], final[:, C : 2 * C]], axis=0)
    gb_v[...] = final[0:1, 2 * C : 3 * C]
    sg_v[...] = sg[...].astype(F32) * (1.0 / math.sqrt(D * YW))
    for c in range(C):
        total = 0.0
        for d in range(D):
            both = su[d, c % H].astype(F32)
            turned = pltpu.roll(both, J, 1)
            both = jnp.where(low, both, turned) if c < H else jnp.where(low, turned, both)
            total = total + both[None] * sg_v[d]
        total = jnp.sum(total, axis=1)
        gm_v[c, :H, :] = total[:, :J]
        gm_v[c, H:, :] = total[:, J:]
    copies = [
        pltpu.make_async_copy(src, dst, g_sem.at[n])
        for n, (src, dst) in enumerate([(gm_v, gm_out), (gp_v, gp_out), (gb_v, gb_out)])
    ]
    for copy in copies:
        copy.start()
    for x in range(XO):
        o_copy(x).wait()
    for copy in copies:
        copy.wait()


def shards(S, D, fields, cotangent, mode_weight, point_weight, bias_vector):
    _, C, XO, YW, Z = fields.shape
    J = mode_weight.shape[2]
    CY = C * YW
    Y = 8 if S == 64 else 2
    A = S // Y
    H = C // 2
    tz = basis_table(S, Z)
    Q = 1
    R = XO // Q
    tx = basis_table(J, S * XO).reshape(J, S, Q, R).swapaxes(1, 2).reshape(J, S * XO)
    tx = np.concatenate([tx, tx], axis=0)
    txt = np.ascontiguousarray(np.concatenate([tx, tx], axis=0).T)
    sizes = (S, D, Y, C, XO, YW, Z, J, Q)
    block = (Q, S, R, CY)
    vmem = pl.BlockSpec(memory_space=pltpu.VMEM)
    hbm = pl.BlockSpec(memory_space=pltpu.HBM)
    dma = pltpu.SemaphoreType.DMA
    shape = jax.ShapeDtypeStruct
    held = pl.pallas_call(
        functools.partial(layer_kernel, sizes),
        out_shape=(
            shape((XO, CY, Z), F32),
            shape(block, BF16),
            shape((D, H, YW, 2 * J), BF16),
            shape((D, H, YW, 2 * J), BF16),
            shape((H, 128), F32),
            shape((S, Z), BF16),
        ),
        in_specs=[hbm] * 8,
        out_specs=(vmem,) * 6,
        scratch_shapes=[
            pltpu.VMEM((XO, C, YW, Z), BF16),
            pltpu.VMEM((XO, C, YW, Z), BF16),
            pltpu.VMEM((XO, CY, Z), BF16),
            pltpu.VMEM((Q, S * R, CY), F32),
            pltpu.VMEM((C, H, 2 * J), F32),
            pltpu.VMEM((C, C, J), F32),
            pltpu.VMEM((C, C), F32),
            pltpu.VMEM((1, C), F32),
            pltpu.VMEM((2 * J, S * XO), BF16),
            pltpu.VMEM((S * XO, 4 * J), BF16),
        ]
        + [pltpu.VMEM(block, BF16)] * 8
        + [
            pltpu.VMEM((D, H, YW, 2 * J), BF16),
            pltpu.VMEM((D, H, YW, 2 * J), BF16),
            pltpu.VMEM((A + Y + D, H, 128), F32),
            dma((XO,)),
            dma((XO,)),
            dma((6,)),
            dma((4 * Q,)),
            dma((4 * Q,)),
            dma((2,)),
            dma((2,)),
            dma((3,)),
            dma((3,)),
        ],
        compiler_params=pltpu.CompilerParams(
            collective_id=0, has_side_effects=True, vmem_limit_bytes=24 * 1024 * 1024
        ),
    )(
        *(
            pltpu.with_memory_space_constraint(operand, pltpu.HBM)
            for operand in (
                fields,
                cotangent,
                mode_weight.reshape(C, C, J),
                point_weight,
                bias_vector.reshape(1, C),
                jnp.asarray(tz),
                jnp.asarray(tx),
                jnp.asarray(txt),
            )
        )
    )
    grad_fields, grad_mode, grad_point, grad_bias = pl.pallas_call(
        functools.partial(result_kernel, sizes),
        out_shape=(
            shape(fields.shape, BF16),
            shape((C, C, J), F32),
            shape((C, C), F32),
            shape((1, C), F32),
        ),
        in_specs=[vmem] * 6,
        out_specs=(hbm,) * 4,
        scratch_shapes=[
            pltpu.VMEM((XO, C, YW, Z), BF16),
            pltpu.VMEM((Q, S * R, CY), F32),
            pltpu.VMEM((D, H, YW, 2 * J), F32),
            pltpu.VMEM((C, C, J), F32),
            pltpu.VMEM((C, C), F32),
            pltpu.VMEM((1, C), F32),
            dma((XO,)),
            dma((3,)),
        ],
        compiler_params=pltpu.CompilerParams(vmem_limit_bytes=24 * 1024 * 1024),
    )(*held)
    return (
        grad_fields,
        grad_mode.reshape(mode_weight.shape),
        grad_point,
        grad_bias.reshape(C),
    )


def solution(mesh):
    return jax.shard_map(
        functools.partial(shards, mesh.shape["space"], mesh.shape["dp"]),
        mesh=mesh,
        in_specs=(
            P("dp", None, "space", None, None),
            P("dp", None, "space", None, None),
            P(None, None, None, "space"),
            P(),
            P(),
        ),
        out_specs=(P("dp", None, "space", None, None), P(None, None, None, "space"), P(), P()),
        check_vma=False,
    )
```

```python
import functools
import math

import jax
import jax.numpy as jnp
import ml_dtypes
import numpy as np
from jax import lax
from jax.experimental import pallas as pl
from jax.experimental.pallas import tpu as pltpu
from jax.sharding import PartitionSpec as P

MESH = pl.DeviceIdType.MESH
F32 = jnp.float32
BF16 = jnp.bfloat16


def basis_table(number, points):
    half = number // 2
    index = np.arange(number)
    freq = np.where(index < half, index, index - half + 1)
    angle = 2.0 * math.pi * ((freq[:, None] * np.arange(points)[None, :]) % points) / points
    values = np.where((index < half)[:, None], np.cos(angle), np.sin(angle))
    values = values * math.sqrt(2.0 / points)
    values[0] = math.sqrt(1.0 / points)
    return values.astype(np.float32).astype(ml_dtypes.bfloat16)


def gelu_slope(value):
    scaled = value * math.sqrt(0.5)
    bell = jnp.exp2(scaled * scaled * (-math.log2(math.e)))
    return 0.5 + 0.5 * lax.erf(scaled) + scaled * (bell * (1.0 / math.sqrt(math.pi)))


def dot(a, b, ca, cb, precision=None):
    return lax.dot_general(
        a, b, (((ca,), (cb,)), ((), ())), precision=precision, preferred_element_type=F32
    )


def split(value):
    high = value.astype(BF16)
    low = (value - high.astype(F32)).astype(BF16)
    return high, low


def layer_kernel(
    sizes, fields, cot, weight_in, point_in, bias_in, tz_in, tx_in, txt_in,
    acc_v, ad_out, su_out, sg_out, sum_out, tz,
    f_v, c_v, g_v, stage, w2, weight, point, bias, tx, txt,
    su_s, su_r, mx_s, mx_r, sg_s, sg_r, ad_s, ad_r,
    du_r, dg_r, pt_r,
    f_sem, c_sem, i_sem, s_sem, r_sem, gs_sem, gr_sem, ps_sem, pr_sem,
):
    S, D, Y, C, XO, YW, Z, J, Q = sizes
    A = S // Y
    X = A // 2
    R = XO // Q
    CY = C * YW
    H = C // 2
    me = lax.axis_index("space")
    dp = lax.axis_index("dp")
    mine_x = me // (2 * Y)
    mine_y = lax.rem(me // 2, Y)
    mine_c = lax.rem(me, 2)

    def f_copy(x):
        return pltpu.make_async_copy(fields.at[0, :, x], f_v.at[x], f_sem.at[x])

    def c_copy(x):
        return pltpu.make_async_copy(cot.at[0, :, x], c_v.at[x], c_sem.at[x])

    small = [
        pltpu.make_async_copy(src, dst, i_sem.at[n])
        for n, (src, dst) in enumerate(
            [(tz_in, tz), (tx_in, tx), (txt_in, txt), (weight_in, weight),
             (point_in, point), (bias_in, bias)]
        )
    ]
    def far_first(act):
        classes = [(a, b) for a in range(X // 2 + 1) for b in range(Y // 2 + 1)]
        for a, b in sorted(classes, key=lambda hops: -sum(hops)):
            ways_x = 1 if 2 * a % X == 0 else 2
            ways_y = 1 if 2 * b % Y == 0 else 2

            @pl.loop(0, 2 * ways_x * ways_y if a + b else 1)
            def _(i):
                turn_x = lax.rem(i // 2, ways_x)
                turn_y = i // (2 * ways_x)
                to_x = lax.rem(mine_x + a + turn_x * (X - 2 * a), X)
                to_y = lax.rem(mine_y + b + turn_y * (Y - 2 * b), Y)
                act((to_x * Y + to_y) * 2 + lax.rem(i, 2) if a + b else me + 1 - 2 * mine_c)

    barrier = pltpu.get_barrier_semaphore()

    @far_first
    def _(to):
        pl.semaphore_signal(barrier, inc=1, device_id={"space": to}, device_id_type=MESH)

    @pl.loop(1, D)
    def _(i):
        pl.semaphore_signal(
            barrier, inc=1, device_id={"dp": lax.rem(dp + i, D)}, device_id_type=MESH
        )

    small[0].start()
    for x in range(XO):
        f_copy(x).start()

    for copy in small[1:]:
        copy.start()
    for x in range(XO):
        c_copy(x).start()

    def send_copy(n, src, dst, to):
        return pltpu.make_async_remote_copy(
            src_ref=src, dst_ref=dst, send_sem=s_sem.at[n], recv_sem=r_sem.at[n],
            device_id={"space": to}, device_id_type=MESH,
        )

    def scatter(n, q, sent, got):
        @far_first
        def _(to):
            send_copy(n * Q + q, sent.at[q, to], got.at[q, me], to).start()

        got[q, pl.ds(me, 1)] = sent[q, pl.ds(me, 1)]

    def all_of(n, q, ref):
        some = ref.at[q, pl.ds(0, S - 1)]
        return send_copy(n * Q + q, some, some, lax.rem(me + 1, S))

    def gather_copy(n, ref, to):
        return pltpu.make_async_remote_copy(
            src_ref=ref, dst_ref=ref, send_sem=gs_sem.at[n], recv_sem=gr_sem.at[n],
            device_id={"dp": to}, device_id_type=MESH,
        )

    def gather(n, ref, value):
        ref[pl.ds(dp, 1)] = value[None]

        @pl.loop(0, D - 1)
        def _(i):
            step = D + D // 2 + ((i + 1) // 2) * (1 - 2 * lax.rem(i, 2))
            gather_copy(n, ref.at[dp], lax.rem(dp + step, D)).start()

    def gather_all(n, ref):
        return gather_copy(n, ref.at[pl.ds(0, D - 1)], lax.rem(dp + 1, D))

    def rows_of(ref, x):
        return ref[x].reshape(CY, Z)

    small[0].wait()
    for q in range(Q):
        for r in range(0, R, 2):
            x = q * R + r
            f_copy(x).wait()
            f_copy(x + 1).wait()
            rows = jnp.concatenate([rows_of(f_v, x), rows_of(f_v, x + 1)], axis=0)
            depth = dot(tz[...], rows, 1, 1)
            for t in range(2):
                stage[q, pl.ds(r + t, S, stride=R), :] = depth[:, t * CY : (t + 1) * CY]
        su_s[q] = stage[q].astype(BF16).reshape(S, R, CY)
        if q == 0:
            pl.semaphore_wait(barrier, S + D - 2)
        scatter(0, q, su_s, su_r)

    for copy in small[1:]:
        copy.wait()
    for c in range(C):
        w2[c] = jnp.concatenate([weight[c, :H, :], weight[c, H:, :]], axis=-1)
    spread = (
        lax.broadcasted_iota(jnp.int32, (CY, C), 0) // YW
        == lax.broadcasted_iota(jnp.int32, (CY, C), 1)
    )
    spread_f = spread.astype(F32)
    spread_b = spread.astype(BF16)
    same = (
        lax.broadcasted_iota(jnp.int32, (CY, CY), 0) % YW
        == lax.broadcasted_iota(jnp.int32, (CY, CY), 1) % YW
    )

    def kron(part, flip):
        rows = dot(spread_b, part, 1, 0 if not flip else 1).astype(BF16)
        return jnp.where(same, dot(rows, spread_b, 1, 1), 0.0).astype(BF16)

    p_high, p_low = split(point[...])
    into_out = jnp.concatenate([kron(p_high, True), kron(p_low, True)], axis=1)
    into_in = jnp.concatenate([kron(p_high, False), kron(p_low, False)], axis=1)
    bias_col = jnp.sum(spread_f * bias[...], axis=1, keepdims=True)

    for x in range(XO):
        rows = rows_of(f_v, x)
        acc_v[x] = dot(into_out, jnp.concatenate([rows, rows], axis=0), 1, 0) + bias_col

    lane = lax.broadcasted_iota(jnp.int32, (H, YW, 2 * J), 2)

    def spectrum(got):
        rows = got[...].reshape(Q * S * R, CY)
        return dot(tx[...], rows, 1, 0).T.reshape(C, YW, 2 * J)

    def back(values):
        high, low = split(values)
        rows = dot(txt[...], jnp.concatenate([high, low], axis=1), 1, 1)
        return rows.astype(BF16).reshape(Q, S, R, CY)

    for q in range(Q):
        all_of(0, q, su_r).wait_recv()
    spec_u = spectrum(su_r)
    mixed = []
    for o in range(H):
        total = w2[0, o : o + 1, :] * spec_u[0]
        for c in range(1, C):
            total = total + w2[c, o : o + 1, :] * spec_u[c]
        mixed.append(total[None])
    mixed = jnp.concatenate(mixed, axis=0)
    mixed = jnp.concatenate(
        [jnp.where(lane < J, mixed, 0.0), jnp.where(lane >= J, mixed, 0.0)], axis=0
    )
    mx_s[...] = back(mixed.reshape(CY, 2 * J))
    for q in range(Q):
        scatter(1, q, mx_s, mx_r)
    gather(0, du_r, jnp.where(lane < J, spec_u[:H], spec_u[H:]).astype(BF16))

    bias_sum = jnp.zeros((1, CY), F32)
    for q in range(Q):
        all_of(1, q, mx_r).wait_recv()
        stage[q] = mx_r[q].reshape(S * R, CY).astype(F32)
        if q == 0:
            for x in range(XO):
                c_copy(x).wait()
        for r in range(R):
            x = q * R + r
            modes = stage[q, pl.ds(r, S, stride=R), :].T.astype(BF16)
            acc_v[x] = acc_v[x] + dot(modes, tz[...], 1, 0)
        for r in range(R):
            x = q * R + r
            g_v[x] = (rows_of(c_v, x).astype(F32) * gelu_slope(acc_v[x])).astype(BF16)
        for r in range(0, R, 2):
            x = q * R + r
            depth = dot(tz[...], jnp.concatenate([g_v[x], g_v[x + 1]], axis=0), 1, 1)
            for t in range(2):
                part = depth[:, t * CY : (t + 1) * CY]
                stage[q, pl.ds(r + t, S, stride=R), :] = part
                bias_sum = bias_sum + part[0:1, :]
        sg_s[q] = stage[q].astype(BF16).reshape(S, R, CY)
        scatter(2, q, sg_s, sg_r)

    pairs = jnp.zeros((CY, CY), F32)
    for x in range(XO):
        pairs = pairs + dot(rows_of(f_v, x), g_v[x], 1, 1)
    pairs = jnp.sum(jnp.where(same, pairs, 0.0).reshape(C, YW, CY), axis=1)
    constant = float(np.float32(ml_dtypes.bfloat16(math.sqrt(1.0 / Z))))
    terms = jnp.concatenate(
        [pairs[:H], pairs[H:], jnp.broadcast_to(bias_sum * (1.0 / constant), (H, CY))], axis=1
    )
    source = lax.broadcasted_iota(jnp.int32, (3 * CY, 128), 0)
    fold = (source // CY) * C + (source % CY) // YW == lax.broadcasted_iota(
        jnp.int32, (3 * CY, 128), 1
    )
    tile = dot(terms, fold.astype(F32), 1, 0, precision=lax.Precision.HIGHEST)

    mine_a = mine_x * 2 + mine_c

    def to_a(a):
        return {"space": ((a // 2) * Y + mine_y) * 2 + lax.rem(a, 2)}

    def to_y(y):
        return {"space": (mine_x * Y + y) * 2 + mine_c}

    def to_dp(d):
        return {"dp": d}

    rounds = [(0, A, mine_a, to_a, 0), (1, Y, mine_y, to_y, A), (2, D, dp, to_dp, A + Y)]

    def p_copy(n, first, last, place):
        return pltpu.make_async_remote_copy(
            src_ref=first, dst_ref=last, send_sem=ps_sem.at[n], recv_sem=pr_sem.at[n],
            device_id=place, device_id_type=MESH,
        )

    def p_send(n, value):
        _, count, mine, place, base = rounds[n]
        pt_r[pl.ds(base + mine, 1)] = value[None]

        @pl.loop(1, count)
        def _(i):
            slot = pt_r.at[base + mine]
            p_copy(n, slot, slot, place(lax.rem(mine + i, count))).start()

    def p_all(n):
        _, count, mine, place, base = rounds[n]
        some = pt_r.at[pl.ds(base, count - 1)]
        return p_copy(n, some, some, place(lax.rem(mine + 1, count)))

    def p_sum(n):
        _, count, _, _, base = rounds[n]
        p_all(n).wait_recv()
        total = pt_r[base]
        for i in range(1, count):
            total = total + pt_r[base + i]
        return total

    p_send(0, tile)
    for x in range(XO):
        rows = g_v[x]
        acc_v[x] = dot(into_in, jnp.concatenate([rows, rows], axis=0), 1, 0)
    p_send(1, p_sum(0))
    gather_all(0, du_r).wait_recv()
    low = lane[0] < J
    for d in range(D):
        for c in range(H):
            both = du_r[d, c].astype(F32)
            turned = pltpu.roll(both, J, 1)
            su_out[d, c] = jnp.where(low, both, turned)
            su_out[d, H + c] = jnp.where(low, turned, both)

    for q in range(Q):
        all_of(2, q, sg_r).wait_recv()
    spec = spectrum(sg_r)
    pair = jnp.where(lane < J, spec[:H], spec[H:])
    gather(1, dg_r, pair.astype(BF16))
    adjoint = []
    for c in range(C):
        total = w2[c, 0:1, :] * pair[0]
        for o in range(1, H):
            total = total + w2[c, o : o + 1, :] * pair[o]
        adjoint.append(total[None])
    ad_s[...] = back(jnp.concatenate(adjoint, axis=0).reshape(CY, 2 * J))
    for q in range(Q):
        scatter(3, q, ad_s, ad_r)
    p_send(2, p_sum(1))

    for q in range(Q):
        all_of(3, q, ad_r).wait_recv()
    ad_out[...] = ad_r[...]
    gather_all(1, dg_r).wait_recv()
    sg_out[...] = dg_r[...]
    sum_out[...] = p_sum(2)

    for q in range(Q):
        for n, sent in enumerate([su_s, mx_s, sg_s, ad_s]):
            all_of(n, q, sent).wait_send()
    for n in range(3):
        p_all(n).wait_send()
    gather_all(0, du_r).wait_send()
    gather_all(1, dg_r).wait_send()


def result_kernel(
    sizes, acc, ad, su, sg, sums, tz,
    out, gm_out, gp_out, gb_out,
    out_v, stage, sg_v, gm_v, gp_v, gb_v, o_sem, g_sem,
):
    S, D, Y, C, XO, YW, Z, J, Q = sizes
    CY = C * YW
    H = C // 2
    R = XO // Q

    def o_copy(x):
        return pltpu.make_async_copy(out_v.at[x], out.at[0, :, x], o_sem.at[x])

    stage[...] = ad[...].reshape(Q, S * R, CY).astype(F32)
    for x in range(XO):
        modes = stage[x // R, pl.ds(x % R, S, stride=R), :].T.astype(BF16)
        grad = acc[x] + dot(modes, tz[...], 1, 0)
        out_v[x] = grad.astype(BF16).reshape(C, YW, Z)
        o_copy(x).start()

    final = sums[...] * (1.0 / math.sqrt(D * S * XO * YW * Z))
    gp_v[...] = jnp.concatenate([final[:, :C], final[:, C : 2 * C]], axis=0)
    gb_v[...] = final[0:1, 2 * C : 3 * C]
    sg_v[...] = sg[...].astype(F32) * (1.0 / math.sqrt(D * YW))
    for c in range(C):
        total = 0.0
        for d in range(D):
            total = total + su[d, c][None] * sg_v[d]
        total = jnp.sum(total, axis=1)
        gm_v[c, :H, :] = total[:, :J]
        gm_v[c, H:, :] = total[:, J:]
    copies = [
        pltpu.make_async_copy(src, dst, g_sem.at[n])
        for n, (src, dst) in enumerate([(gm_v, gm_out), (gp_v, gp_out), (gb_v, gb_out)])
    ]
    for copy in copies:
        copy.start()
    for x in range(XO):
        o_copy(x).wait()
    for copy in copies:
        copy.wait()


def shards(S, D, fields, cotangent, mode_weight, point_weight, bias_vector):
    _, C, XO, YW, Z = fields.shape
    J = mode_weight.shape[2]
    CY = C * YW
    Y = 8 if S == 64 else 2
    A = S // Y
    H = C // 2
    tz = basis_table(S, Z)
    Q = 1
    R = XO // Q
    tx = basis_table(J, S * XO).reshape(J, S, Q, R).swapaxes(1, 2).reshape(J, S * XO)
    tx = np.concatenate([tx, tx], axis=0)
    txt = np.ascontiguousarray(np.concatenate([tx, tx], axis=0).T)
    sizes = (S, D, Y, C, XO, YW, Z, J, Q)
    block = (Q, S, R, CY)
    vmem = pl.BlockSpec(memory_space=pltpu.VMEM)
    hbm = pl.BlockSpec(memory_space=pltpu.HBM)
    dma = pltpu.SemaphoreType.DMA
    shape = jax.ShapeDtypeStruct
    held = pl.pallas_call(
        functools.partial(layer_kernel, sizes),
        out_shape=(
            shape((XO, CY, Z), F32),
            shape(block, BF16),
            shape((D, C, YW, 2 * J), F32),
            shape((D, H, YW, 2 * J), BF16),
            shape((H, 128), F32),
            shape((S, Z), BF16),
        ),
        in_specs=[hbm] * 8,
        out_specs=(vmem,) * 6,
        scratch_shapes=[
            pltpu.VMEM((XO, C, YW, Z), BF16),
            pltpu.VMEM((XO, C, YW, Z), BF16),
            pltpu.VMEM((XO, CY, Z), BF16),
            pltpu.VMEM((Q, S * R, CY), F32),
            pltpu.VMEM((C, H, 2 * J), F32),
            pltpu.VMEM((C, C, J), F32),
            pltpu.VMEM((C, C), F32),
            pltpu.VMEM((1, C), F32),
            pltpu.VMEM((2 * J, S * XO), BF16),
            pltpu.VMEM((S * XO, 4 * J), BF16),
        ]
        + [pltpu.VMEM(block, BF16)] * 8
        + [
            pltpu.VMEM((D, H, YW, 2 * J), BF16),
            pltpu.VMEM((D, H, YW, 2 * J), BF16),
            pltpu.VMEM((A + Y + D, H, 128), F32),
            dma((XO,)),
            dma((XO,)),
            dma((6,)),
            dma((4 * Q,)),
            dma((4 * Q,)),
            dma((2,)),
            dma((2,)),
            dma((3,)),
            dma((3,)),
        ],
        compiler_params=pltpu.CompilerParams(
            collective_id=0, has_side_effects=True, vmem_limit_bytes=24 * 1024 * 1024
        ),
    )(
        *(
            pltpu.with_memory_space_constraint(operand, pltpu.HBM)
            for operand in (
                fields,
                cotangent,
                mode_weight.reshape(C, C, J),
                point_weight,
                bias_vector.reshape(1, C),
                jnp.asarray(tz),
                jnp.asarray(tx),
                jnp.asarray(txt),
            )
        )
    )
    grad_fields, grad_mode, grad_point, grad_bias = pl.pallas_call(
        functools.partial(result_kernel, sizes),
        out_shape=(
            shape(fields.shape, BF16),
            shape((C, C, J), F32),
            shape((C, C), F32),
            shape((1, C), F32),
        ),
        in_specs=[vmem] * 6,
        out_specs=(hbm,) * 4,
        scratch_shapes=[
            pltpu.VMEM((XO, C, YW, Z), BF16),
            pltpu.VMEM((Q, S * R, CY), F32),
            pltpu.VMEM((D, H, YW, 2 * J), F32),
            pltpu.VMEM((C, C, J), F32),
            pltpu.VMEM((C, C), F32),
            pltpu.VMEM((1, C), F32),
            dma((XO,)),
            dma((3,)),
        ],
        compiler_params=pltpu.CompilerParams(vmem_limit_bytes=24 * 1024 * 1024),
    )(*held)
    return (
        grad_fields,
        grad_mode.reshape(mode_weight.shape),
        grad_point,
        grad_bias.reshape(C),
    )


def solution(mesh):
    return jax.shard_map(
        functools.partial(shards, mesh.shape["space"], mesh.shape["dp"]),
        mesh=mesh,
        in_specs=(
            P("dp", None, "space", None, None),
            P("dp", None, "space", None, None),
            P(None, None, None, "space"),
            P(),
            P(),
        ),
        out_specs=(P("dp", None, "space", None, None), P(None, None, None, "space"), P(), P()),
        check_vma=False,
    )
```

```python
import functools
import math

import jax
import jax.numpy as jnp
import ml_dtypes
import numpy as np
from jax import lax
from jax.experimental import pallas as pl
from jax.experimental.pallas import tpu as pltpu
from jax.sharding import PartitionSpec as P

MESH = pl.DeviceIdType.MESH
F32 = jnp.float32
BF16 = jnp.bfloat16


def basis_table(number, points):
    half = number // 2
    index = np.arange(number)
    freq = np.where(index < half, index, index - half + 1)
    angle = 2.0 * math.pi * ((freq[:, None] * np.arange(points)[None, :]) % points) / points
    values = np.where((index < half)[:, None], np.cos(angle), np.sin(angle))
    values = values * math.sqrt(2.0 / points)
    values[0] = math.sqrt(1.0 / points)
    return values.astype(np.float32).astype(ml_dtypes.bfloat16)


def gelu_slope(value):
    scaled = value * math.sqrt(0.5)
    bell = jnp.exp2(scaled * scaled * (-math.log2(math.e)))
    return 0.5 + 0.5 * lax.erf(scaled) + scaled * (bell * (1.0 / math.sqrt(math.pi)))


def dot(a, b, ca, cb, precision=None):
    return lax.dot_general(
        a, b, (((ca,), (cb,)), ((), ())), precision=precision, preferred_element_type=F32
    )


def split(value):
    high = value.astype(BF16)
    low = (value - high.astype(F32)).astype(BF16)
    return high, low


def layer_kernel(
    sizes, fields, cot, weight_in, point_in, bias_in, tz_in, tx_in, txt_in,
    acc_v, ad_out, su_out, sg_out, sum_out, tz,
    f_v, c_v, g_v, stage, w2, weight, point, bias, tx, txt,
    su_s, su_r, mx_s, mx_r, sg_s, sg_r, ad_s, ad_r,
    du_r, dg_r, pt_r,
    f_sem, c_sem, i_sem, s_sem, r_sem, gs_sem, gr_sem, ps_sem, pr_sem,
):
    S, D, Y, C, XO, YW, Z, J, Q = sizes
    A = S // Y
    X = A // 2
    R = XO // Q
    CY = C * YW
    H = C // 2
    me = lax.axis_index("space")
    dp = lax.axis_index("dp")
    mine_x = me // (2 * Y)
    mine_y = lax.rem(me // 2, Y)
    mine_c = lax.rem(me, 2)

    def f_copy(x):
        return pltpu.make_async_copy(fields.at[0, :, x], f_v.at[x], f_sem.at[x])

    def c_copy(x):
        return pltpu.make_async_copy(cot.at[0, :, x], c_v.at[x], c_sem.at[x])

    small = [
        pltpu.make_async_copy(src, dst, i_sem.at[n])
        for n, (src, dst) in enumerate(
            [(tz_in, tz), (tx_in, tx), (txt_in, txt), (weight_in, weight),
             (point_in, point), (bias_in, bias)]
        )
    ]
    def far_first(act):
        classes = [(a, b) for a in range(X // 2 + 1) for b in range(Y // 2 + 1)]
        for a, b in sorted(classes, key=lambda hops: -sum(hops)):
            ways_x = 1 if 2 * a % X == 0 else 2
            ways_y = 1 if 2 * b % Y == 0 else 2

            @pl.loop(0, 2 * ways_x * ways_y if a + b else 1)
            def _(i):
                turn_x = lax.rem(i // 2, ways_x)
                turn_y = i // (2 * ways_x)
                to_x = lax.rem(mine_x + a + turn_x * (X - 2 * a), X)
                to_y = lax.rem(mine_y + b + turn_y * (Y - 2 * b), Y)
                act((to_x * Y + to_y) * 2 + lax.rem(i, 2) if a + b else me + 1 - 2 * mine_c)

    barrier = pltpu.get_barrier_semaphore()

    @far_first
    def _(to):
        pl.semaphore_signal(barrier, inc=1, device_id={"space": to}, device_id_type=MESH)

    @pl.loop(1, D)
    def _(i):
        pl.semaphore_signal(
            barrier, inc=1, device_id={"dp": lax.rem(dp + i, D)}, device_id_type=MESH
        )

    small[0].start()
    for x in range(XO):
        f_copy(x).start()

    for copy in small[1:]:
        copy.start()
    for x in range(XO):
        c_copy(x).start()

    def send_copy(n, src, dst, to):
        return pltpu.make_async_remote_copy(
            src_ref=src, dst_ref=dst, send_sem=s_sem.at[n], recv_sem=r_sem.at[n],
            device_id={"space": to}, device_id_type=MESH,
        )

    def scatter(n, q, sent, got):
        @far_first
        def _(to):
            send_copy(n * Q + q, sent.at[q, to], got.at[q, me], to).start()

        got[q, pl.ds(me, 1)] = sent[q, pl.ds(me, 1)]

    def all_of(n, q, ref):
        some = ref.at[q, pl.ds(0, S - 1)]
        return send_copy(n * Q + q, some, some, lax.rem(me + 1, S))

    def gather_copy(n, ref, to):
        return pltpu.make_async_remote_copy(
            src_ref=ref, dst_ref=ref, send_sem=gs_sem.at[n], recv_sem=gr_sem.at[n],
            device_id={"dp": to}, device_id_type=MESH,
        )

    def gather(n, ref, value):
        ref[pl.ds(dp, 1)] = value[None]

        @pl.loop(0, D - 1)
        def _(i):
            step = D + D // 2 + ((i + 1) // 2) * (1 - 2 * lax.rem(i, 2))
            gather_copy(n, ref.at[dp], lax.rem(dp + step, D)).start()

    def gather_all(n, ref):
        return gather_copy(n, ref.at[pl.ds(0, D - 1)], lax.rem(dp + 1, D))

    def rows_of(ref, x):
        return ref[x].reshape(CY, Z)

    small[0].wait()
    for q in range(Q):
        for r in range(0, R, 4):
            x = q * R + r
            for t in range(4):
                f_copy(x + t).wait()
            rows = f_v[pl.ds(x, 4)].reshape(4 * CY, Z)
            depth = dot(tz[...], rows, 1, 1)
            for t in range(4):
                stage[q, pl.ds(r + t, S, stride=R), :] = depth[:, t * CY : (t + 1) * CY]
        su_s[q] = stage[q].astype(BF16).reshape(S, R, CY)
        if q == 0:
            pl.semaphore_wait(barrier, S + D - 2)
        scatter(0, q, su_s, su_r)

    for copy in small[1:]:
        copy.wait()
    for c in range(C):
        w2[c] = jnp.concatenate([weight[c, :H, :], weight[c, H:, :]], axis=-1)
    spread = (
        lax.broadcasted_iota(jnp.int32, (CY, C), 0) // YW
        == lax.broadcasted_iota(jnp.int32, (CY, C), 1)
    )
    spread_f = spread.astype(F32)
    spread_b = spread.astype(BF16)
    same = (
        lax.broadcasted_iota(jnp.int32, (CY, CY), 0) % YW
        == lax.broadcasted_iota(jnp.int32, (CY, CY), 1) % YW
    )

    def kron(part, flip):
        rows = dot(spread_b, part, 1, 0 if not flip else 1).astype(BF16)
        return jnp.where(same, dot(rows, spread_b, 1, 1), 0.0).astype(BF16)

    p_high, p_low = split(point[...])
    into_out = jnp.concatenate([kron(p_high, True), kron(p_low, True)], axis=1)
    into_in = jnp.concatenate([kron(p_high, False), kron(p_low, False)], axis=1)
    bias_col = jnp.sum(spread_f * bias[...], axis=1, keepdims=True)

    for x in range(XO):
        rows = rows_of(f_v, x)
        acc_v[x] = dot(into_out, jnp.concatenate([rows, rows], axis=0), 1, 0) + bias_col

    lane = lax.broadcasted_iota(jnp.int32, (H, YW, 2 * J), 2)

    def spectrum(got):
        rows = got[...].reshape(Q * S * R, CY)
        return dot(tx[...], rows, 1, 0).T.reshape(C, YW, 2 * J)

    def back(values):
        high, low = split(values)
        rows = dot(txt[...], jnp.concatenate([high, low], axis=1), 1, 1)
        return rows.astype(BF16).reshape(Q, S, R, CY)

    for q in range(Q):
        all_of(0, q, su_r).wait_recv()
    spec_u = spectrum(su_r)
    mixed = []
    for o in range(H):
        total = w2[0, o : o + 1, :] * spec_u[0]
        for c in range(1, C):
            total = total + w2[c, o : o + 1, :] * spec_u[c]
        mixed.append(total[None])
    mixed = jnp.concatenate(mixed, axis=0)
    mixed = jnp.concatenate(
        [jnp.where(lane < J, mixed, 0.0), jnp.where(lane >= J, mixed, 0.0)], axis=0
    )
    mx_s[...] = back(mixed.reshape(CY, 2 * J))
    for q in range(Q):
        scatter(1, q, mx_s, mx_r)
    gather(0, du_r, jnp.where(lane < J, spec_u[:H], spec_u[H:]).astype(BF16))

    bias_sum = jnp.zeros((1, CY), F32)
    for q in range(Q):
        all_of(1, q, mx_r).wait_recv()
        stage[q] = mx_r[q].reshape(S * R, CY).astype(F32)
        if q == 0:
            for x in range(XO):
                c_copy(x).wait()
        for r in range(R):
            x = q * R + r
            modes = stage[q, pl.ds(r, S, stride=R), :].T.astype(BF16)
            acc_v[x] = acc_v[x] + dot(modes, tz[...], 1, 0)
        for r in range(R):
            x = q * R + r
            g_v[x] = (rows_of(c_v, x).astype(F32) * gelu_slope(acc_v[x])).astype(BF16)
        for r in range(0, R, 4):
            x = q * R + r
            depth = dot(tz[...], g_v[pl.ds(x, 4)].reshape(4 * CY, Z), 1, 1)
            for t in range(4):
                part = depth[:, t * CY : (t + 1) * CY]
                stage[q, pl.ds(r + t, S, stride=R), :] = part
                bias_sum = bias_sum + part[0:1, :]
        sg_s[q] = stage[q].astype(BF16).reshape(S, R, CY)
        scatter(2, q, sg_s, sg_r)

    pairs = jnp.zeros((CY, CY), F32)
    for x in range(XO):
        pairs = pairs + dot(rows_of(f_v, x), g_v[x], 1, 1)
    pairs = jnp.sum(jnp.where(same, pairs, 0.0).reshape(C, YW, CY), axis=1)
    constant = float(np.float32(ml_dtypes.bfloat16(math.sqrt(1.0 / Z))))
    terms = jnp.concatenate(
        [pairs[:H], pairs[H:], jnp.broadcast_to(bias_sum * (1.0 / constant), (H, CY))], axis=1
    )
    source = lax.broadcasted_iota(jnp.int32, (3 * CY, 128), 0)
    fold = (source // CY) * C + (source % CY) // YW == lax.broadcasted_iota(
        jnp.int32, (3 * CY, 128), 1
    )
    tile = dot(terms, fold.astype(F32), 1, 0, precision=lax.Precision.HIGHEST)

    mine_a = mine_x * 2 + mine_c

    def to_a(a):
        return {"space": ((a // 2) * Y + mine_y) * 2 + lax.rem(a, 2)}

    def to_y(y):
        return {"space": (mine_x * Y + y) * 2 + mine_c}

    def to_dp(d):
        return {"dp": d}

    rounds = [(0, A, mine_a, to_a, 0), (1, Y, mine_y, to_y, A), (2, D, dp, to_dp, A + Y)]

    def p_copy(n, first, last, place):
        return pltpu.make_async_remote_copy(
            src_ref=first, dst_ref=last, send_sem=ps_sem.at[n], recv_sem=pr_sem.at[n],
            device_id=place, device_id_type=MESH,
        )

    def p_send(n, value):
        _, count, mine, place, base = rounds[n]
        pt_r[pl.ds(base + mine, 1)] = value[None]

        @pl.loop(1, count)
        def _(i):
            slot = pt_r.at[base + mine]
            p_copy(n, slot, slot, place(lax.rem(mine + i, count))).start()

    def p_all(n):
        _, count, mine, place, base = rounds[n]
        some = pt_r.at[pl.ds(base, count - 1)]
        return p_copy(n, some, some, place(lax.rem(mine + 1, count)))

    def p_sum(n):
        _, count, _, _, base = rounds[n]
        p_all(n).wait_recv()
        total = pt_r[base]
        for i in range(1, count):
            total = total + pt_r[base + i]
        return total

    p_send(0, tile)
    for x in range(XO):
        rows = g_v[x]
        acc_v[x] = dot(into_in, jnp.concatenate([rows, rows], axis=0), 1, 0)
    p_send(1, p_sum(0))
    gather_all(0, du_r).wait_recv()
    low = lane[0] < J
    for d in range(D):
        for c in range(H):
            both = du_r[d, c].astype(F32)
            turned = pltpu.roll(both, J, 1)
            su_out[d, c] = jnp.where(low, both, turned)
            su_out[d, H + c] = jnp.where(low, turned, both)

    for q in range(Q):
        all_of(2, q, sg_r).wait_recv()
    spec = spectrum(sg_r)
    pair = jnp.where(lane < J, spec[:H], spec[H:])
    gather(1, dg_r, pair.astype(BF16))
    adjoint = []
    for c in range(C):
        total = w2[c, 0:1, :] * pair[0]
        for o in range(1, H):
            total = total + w2[c, o : o + 1, :] * pair[o]
        adjoint.append(total[None])
    ad_s[...] = back(jnp.concatenate(adjoint, axis=0).reshape(CY, 2 * J))
    for q in range(Q):
        scatter(3, q, ad_s, ad_r)
    p_send(2, p_sum(1))

    for q in range(Q):
        all_of(3, q, ad_r).wait_recv()
    ad_out[...] = ad_r[...]
    gather_all(1, dg_r).wait_recv()
    sg_out[...] = dg_r[...]
    sum_out[...] = p_sum(2)

    for q in range(Q):
        for n, sent in enumerate([su_s, mx_s, sg_s, ad_s]):
            all_of(n, q, sent).wait_send()
    for n in range(3):
        p_all(n).wait_send()
    gather_all(0, du_r).wait_send()
    gather_all(1, dg_r).wait_send()


def result_kernel(
    sizes, acc, ad, su, sg, sums, tz,
    out, gm_out, gp_out, gb_out,
    out_v, stage, sg_v, gm_v, gp_v, gb_v, o_sem, g_sem,
):
    S, D, Y, C, XO, YW, Z, J, Q = sizes
    CY = C * YW
    H = C // 2
    R = XO // Q

    def o_copy(x):
        return pltpu.make_async_copy(out_v.at[x], out.at[0, :, x], o_sem.at[x])

    stage[...] = ad[...].reshape(Q, S * R, CY).astype(F32)
    for x in range(XO):
        modes = stage[x // R, pl.ds(x % R, S, stride=R), :].T.astype(BF16)
        grad = acc[x] + dot(modes, tz[...], 1, 0)
        out_v[x] = grad.astype(BF16).reshape(C, YW, Z)
        o_copy(x).start()

    final = sums[...] * (1.0 / math.sqrt(D * S * XO * YW * Z))
    gp_v[...] = jnp.concatenate([final[:, :C], final[:, C : 2 * C]], axis=0)
    gb_v[...] = final[0:1, 2 * C : 3 * C]
    sg_v[...] = sg[...].astype(F32) * (1.0 / math.sqrt(D * YW))
    for c in range(C):
        total = 0.0
        for d in range(D):
            total = total + su[d, c][None] * sg_v[d]
        total = jnp.sum(total, axis=1)
        gm_v[c, :H, :] = total[:, :J]
        gm_v[c, H:, :] = total[:, J:]
    copies = [
        pltpu.make_async_copy(src, dst, g_sem.at[n])
        for n, (src, dst) in enumerate([(gm_v, gm_out), (gp_v, gp_out), (gb_v, gb_out)])
    ]
    for copy in copies:
        copy.start()
    for x in range(XO):
        o_copy(x).wait()
    for copy in copies:
        copy.wait()


def shards(S, D, fields, cotangent, mode_weight, point_weight, bias_vector):
    _, C, XO, YW, Z = fields.shape
    J = mode_weight.shape[2]
    CY = C * YW
    Y = 8 if S == 64 else 2
    A = S // Y
    H = C // 2
    tz = basis_table(S, Z)
    Q = 1
    R = XO // Q
    tx = basis_table(J, S * XO).reshape(J, S, Q, R).swapaxes(1, 2).reshape(J, S * XO)
    tx = np.concatenate([tx, tx], axis=0)
    txt = np.ascontiguousarray(np.concatenate([tx, tx], axis=0).T)
    sizes = (S, D, Y, C, XO, YW, Z, J, Q)
    block = (Q, S, R, CY)
    vmem = pl.BlockSpec(memory_space=pltpu.VMEM)
    hbm = pl.BlockSpec(memory_space=pltpu.HBM)
    dma = pltpu.SemaphoreType.DMA
    shape = jax.ShapeDtypeStruct
    held = pl.pallas_call(
        functools.partial(layer_kernel, sizes),
        out_shape=(
            shape((XO, CY, Z), F32),
            shape(block, BF16),
            shape((D, C, YW, 2 * J), F32),
            shape((D, H, YW, 2 * J), BF16),
            shape((H, 128), F32),
            shape((S, Z), BF16),
        ),
        in_specs=[hbm] * 8,
        out_specs=(vmem,) * 6,
        scratch_shapes=[
            pltpu.VMEM((XO, C, YW, Z), BF16),
            pltpu.VMEM((XO, C, YW, Z), BF16),
            pltpu.VMEM((XO, CY, Z), BF16),
            pltpu.VMEM((Q, S * R, CY), F32),
            pltpu.VMEM((C, H, 2 * J), F32),
            pltpu.VMEM((C, C, J), F32),
            pltpu.VMEM((C, C), F32),
            pltpu.VMEM((1, C), F32),
            pltpu.VMEM((2 * J, S * XO), BF16),
            pltpu.VMEM((S * XO, 4 * J), BF16),
        ]
        + [pltpu.VMEM(block, BF16)] * 8
        + [
            pltpu.VMEM((D, H, YW, 2 * J), BF16),
            pltpu.VMEM((D, H, YW, 2 * J), BF16),
            pltpu.VMEM((A + Y + D, H, 128), F32),
            dma((XO,)),
            dma((XO,)),
            dma((6,)),
            dma((4 * Q,)),
            dma((4 * Q,)),
            dma((2,)),
            dma((2,)),
            dma((3,)),
            dma((3,)),
        ],
        compiler_params=pltpu.CompilerParams(
            collective_id=0, has_side_effects=True, vmem_limit_bytes=24 * 1024 * 1024
        ),
    )(
        *(
            pltpu.with_memory_space_constraint(operand, pltpu.HBM)
            for operand in (
                fields,
                cotangent,
                mode_weight.reshape(C, C, J),
                point_weight,
                bias_vector.reshape(1, C),
                jnp.asarray(tz),
                jnp.asarray(tx),
                jnp.asarray(txt),
            )
        )
    )
    grad_fields, grad_mode, grad_point, grad_bias = pl.pallas_call(
        functools.partial(result_kernel, sizes),
        out_shape=(
            shape(fields.shape, BF16),
            shape((C, C, J), F32),
            shape((C, C), F32),
            shape((1, C), F32),
        ),
        in_specs=[vmem] * 6,
        out_specs=(hbm,) * 4,
        scratch_shapes=[
            pltpu.VMEM((XO, C, YW, Z), BF16),
            pltpu.VMEM((Q, S * R, CY), F32),
            pltpu.VMEM((D, H, YW, 2 * J), F32),
            pltpu.VMEM((C, C, J), F32),
            pltpu.VMEM((C, C), F32),
            pltpu.VMEM((1, C), F32),
            dma((XO,)),
            dma((3,)),
        ],
        compiler_params=pltpu.CompilerParams(vmem_limit_bytes=24 * 1024 * 1024),
    )(*held)
    return (
        grad_fields,
        grad_mode.reshape(mode_weight.shape),
        grad_point,
        grad_bias.reshape(C),
    )


def solution(mesh):
    return jax.shard_map(
        functools.partial(shards, mesh.shape["space"], mesh.shape["dp"]),
        mesh=mesh,
        in_specs=(
            P("dp", None, "space", None, None),
            P("dp", None, "space", None, None),
            P(None, None, None, "space"),
            P(),
            P(),
        ),
        out_specs=(P("dp", None, "space", None, None), P(None, None, None, "space"), P(), P()),
        check_vma=False,
    )
```
